512 devices in a mesh: pole: 16 (over y, x_hi, core), grid: 32 (over z, x_lo).
Axes of the slice: x: 4 (x_hi: 2, x_lo: 2; x = x_hi * 2 + x_lo), y: 4, z: 16, core: 2. Of those that a mesh axis runs over, the one named last changes fastest.
Arguments:
- panel: bfloat16 [16, 2, 2048, 1024], P('pole', None, 'grid'), may hold values from -0.25 to 0.25
- inverse_blocks: bfloat16 [16, 32, 8, 2, 64, 64], P('pole', 'grid'), may hold values from -6 to 6
- diag_inverse: float32 [16, 1024, 2048], P('pole', 'grid'), may hold values from -6 to 6
- ancestors: int32 [32, 8], P('grid'), may hold values from 0 to 31, all different within a row
- pole_index: int32 [16], P('pole'), may hold values from 0 to 63
- weight_table: float32 [64, 2], replicated, may hold values from -1 to 1
Outputs:
- offdiag: bfloat16 [16, 2, 2048, 1024], P('pole', None, 'grid')
- density: float32 [1024, 1024], P('grid')
The draws below stay inside these ranges and needn't reach their ends.
All inputs are finite; a program needn't handle non-finite values.
Results may differ from the reference program's by a relative error of at most 0.0007.
Values may be sent and summed in bfloat16 or wider, within the bound.
A program may use at most 64 MiB of HBM per device.

```python
import jax
import jax.numpy as jnp
from jax import lax

W = 1024
B = 64
KA = 8
NW = 64
NB = 32
M = 2048
NPOLE = 16


def plant(result, key, least, high):
    longest = result.shape.index(max(result.shape))
    spots = []
    for shift in (0, 1):
        where = [jax.random.randint(jax.random.fold_in(key, axis), (), 0, length) for axis, length in enumerate(result.shape)]
        where[longest] = (where[longest] + shift) % result.shape[longest]
        spots.append(tuple(where))
    return result.at[spots[0]].set(least).at[spots[1]].set(high)


def block_levels(stream_key, extent, cuts, smallest, top_value):
    level, own = 1.0, jax.random.fold_in(stream_key, 6)
    for axis_at, parts in cuts:
        draws = jnp.exp(jax.random.uniform(jax.random.fold_in(own, axis_at), (parts,), jnp.float32, smallest / len(cuts), top_value / len(cuts)))
        level = level * jnp.repeat(draws, extent[axis_at] // parts).reshape([-1 if axis == axis_at else 1 for axis in range(len(extent))])
    return level


def picks_of(key, rows, count, top, lift):
    ranking = jax.random.permutation(jax.random.fold_in(key, 1), count)
    favour = ranking
    for power in range(3):
        favour = favour * favour // count
    favour = favour * lift // count
    chance = jax.random.randint(jax.random.fold_in(key, 2), (rows, count), 0, 4096) + favour
    holders = jax.random.permutation(jax.random.fold_in(key, 3), rows)[jnp.arange(count) % rows]
    chance = jnp.where(jnp.arange(rows)[:, None] == holders[None, :], 1 << 14, chance)
    priority = chance * count + jnp.arange(count)
    return lax.top_k(priority.astype(jnp.int32), top)[1].astype(jnp.int32)


def centred(key, dims, spread, most, shards=(), kind=jnp.bfloat16):
    loudness = block_levels(key, dims, shards, -0.22, 0.18) if shards else 1.0
    entries = jax.random.normal(key, dims, jnp.float32) * spread * loudness
    return jnp.minimum(jnp.maximum(entries, -most), most).astype(kind)


def setup_inputs(seed: int = 0) -> dict:
    streams_of = jax.random.split(jax.random.key(seed), 7)
    panel = centred(streams_of[0], (NPOLE, 2, M, W), ((2 * M) ** -0.5), 0.25, ((0, 16), (2, 32)))
    inverse_blocks = centred(streams_of[1], (NPOLE, NB, KA, 2, B, B), ((NB / KA) ** 0.5), 6.0, ((0, 16), (1, 32)))
    diag_inverse = centred(streams_of[2], (NPOLE, W, 2 * W), 1.0, 6.0, ((0, 16), (1, 32)), jnp.float32)
    ancestors = picks_of(streams_of[3], NB, NB, KA, 4096)
    pole_index = plant(jax.random.randint(streams_of[4], (NPOLE,), 0, NW), jax.random.fold_in(streams_of[4], 1), 0, NW - 1).astype(jnp.int32)
    weight_table = jnp.clip(jax.random.uniform(streams_of[5], (NW, 2), jnp.float32, -1.0, 1.0), -1.0, 1.0)
    return dict(panel=panel, inverse_blocks=inverse_blocks, diag_inverse=diag_inverse, ancestors=ancestors, pole_index=pole_index, weight_table=weight_table)


def pole_front(panel_p, blocks_p, dinv_p, ancestors, weights):
    blocks = panel_p.astype(jnp.float32).reshape(2, NB, B, W)
    chosen = blocks[:, ancestors]
    inverse = blocks_p.astype(jnp.float32)

    def times(left, right):
        return jnp.einsum('ikab,ikbw->iaw', left, right)

    real_part = -(times(inverse[:, :, 0], chosen[0]) - times(inverse[:, :, 1], chosen[1]))
    imag_part = -(times(inverse[:, :, 0], chosen[1]) + times(inverse[:, :, 1], chosen[0]))
    product_p = jnp.stack([real_part, imag_part])
    offdiag_p = product_p.astype(jnp.bfloat16)
    panel_rows = panel_p.astype(jnp.float32).reshape(2, NB, B, W).transpose(1, 0, 2, 3)
    off_rows = product_p.transpose(1, 0, 2, 3)
    high = lax.Precision.HIGHEST

    def accumulate(total, pair):
        lrow, xrow = pair
        term_real = jnp.dot(lrow[0].T, xrow[0], precision=high) - jnp.dot(lrow[1].T, xrow[1], precision=high)
        term_imag = jnp.dot(lrow[0].T, xrow[1], precision=high) + jnp.dot(lrow[1].T, xrow[0], precision=high)
        term = weights[0] * term_real - weights[1] * term_imag
        return total + term, None

    total, _ = lax.scan(accumulate, jnp.zeros((W, W), jnp.float32), (panel_rows, off_rows))
    own = weights[0] * dinv_p[:, :W] - weights[1] * dinv_p[:, W:]
    return offdiag_p.reshape(2, M, W), own - total


def reference(panel, inverse_blocks, diag_inverse, ancestors, pole_index, weight_table):
    results = []
    density = jnp.zeros((W, W), jnp.float32)
    for pole in range(NPOLE):
        weights = weight_table[pole_index[pole]]
        offdiag_p, part = pole_front(panel[pole], inverse_blocks[pole], diag_inverse[pole], ancestors, weights)
        results.append(offdiag_p)
        density = density + part
    return jnp.stack(results), density
```

```python
import functools

import jax
import jax.numpy as jnp
from jax import lax
from jax.experimental import pallas as pl
from jax.experimental.pallas import tpu as pltpu
from jax.sharding import PartitionSpec as P

MESH = pl.DeviceIdType.MESH
F32 = jnp.float32
BF16 = jnp.bfloat16
WAVES = 2
COLS = 512 // WAVES
LAG = (0, 1)
STEPS = 8


def kernel(
    anc_s, pole_s, table_s, panel, inv, diag, anc_v,
    off, dens,
    b00, b01, b10, b11, left_own, left_par, ancp_v, ancp_s, prow, pt, xs, xo,
    d0, d1, rc0, rc1, e0, e1, ry0, ry1, f0, f1, rz0, rz1, wd, dg, res,
    loc_sem, xc_send, xc_recv, misc_send, misc_recv, small_sem,
    ring_send, ring_recv, xo_send, xo_recv, c_send, c_recv, y_send, y_recv,
    z_send, z_recv, g_send, g_recv, n_send, n_recv,
):
    bufs = ((b00, b01), (b10, b11))
    ds, rcs, es, rys, fs, rzs = (d0, d1), (rc0, rc1), (e0, e1), (ry0, ry1), (f0, f1), (rz0, rz1)
    g = lax.axis_index("grid")
    p = lax.axis_index("pole")
    z, xl = g // 2, g % 2
    y, xh, core = p // 4, (p // 2) % 2, p % 2
    gx = 2 * z + 1 - xl
    gr = 2 * lax.rem(z + 1, 16) + xl
    gl = 2 * lax.rem(z + 15, 16) + xl
    pc = p + 1 - 2 * core
    xh_own = z // 8
    owner = xh == xh_own
    own = jnp.where(owner, 1, 0)
    own_self = jnp.where(jnp.logical_and(owner, core == xl), 1, 0)

    def at(pole, grid):
        return {"pole": pole, "grid": grid}

    def remote(src, dst, send, recv, pole, grid):
        return pltpu.make_async_remote_copy(
            src_ref=src, dst_ref=dst, send_sem=send, recv_sem=recv,
            device_id=at(pole, grid), device_id_type=MESH,
        )

    barrier = pltpu.get_barrier_semaphore()

    def hello(pole, grid):
        pl.semaphore_signal(barrier, inc=1, device_id=at(pole, grid), device_id_type=MESH)

    hello(p, gx)
    hello(p, gr)
    hello(p, gl)
    hello(pc, g)
    for k in range(1, 4):
        hello(lax.rem(y + k, 4) * 4 + xh * 2 + core, g)

    def not_me(pole, grid):
        return jnp.logical_or(pole != p, grid != g)

    def owner_of(n):
        return (n // 2) * 4 + xh_own * 2 + xl, 2 * z + n % 2

    def source(n):
        return y * 4 + (n // 16) * 2 + core, 2 * lax.rem(n, 16) + xl

    def to_final(n, carry):
        pole, grid = owner_of(n)

        @pl.when(not_me(pole, grid))
        def _():
            hello(pole, grid)

        return carry

    lax.fori_loop(0, 8, to_final, 0)

    @pl.when(owner)
    def _():
        def to_source(n, carry):
            pole, grid = source(n)

            @pl.when(not_me(pole, grid))
            def _():
                hello(pole, grid)

            return carry

        lax.fori_loop(0, 32, to_source, 0)

        def to_diag(n, carry):
            @pl.when(not_me(n, 2 * z + core))
            def _():
                hello(n, 2 * z + core)

            return carry

        lax.fori_loop(0, 16, to_diag, 0)

    index = pole_s[0]
    wr = table_s[index, 0]
    wi = table_s[index, 1]
    for k in range(0, 8, 2):
        left_own[:, 64 * k : 64 * k + 128] = jnp.concatenate(
            [inv[0, 0, k].reshape(128, 64), inv[0, 0, k + 1].reshape(128, 64)], axis=1
        )
    for h in range(2):
        wd[h] = wr * diag[0, :, 512 * h : 512 * h + 512] - wi * diag[0, :, 1024 + 512 * h : 1536 + 512 * h]

    def transpose_rows(rows, at_lane):
        for n in range(4):
            part = rows[:, :, 256 * n : 256 * n + 256].reshape(128, 256).astype(F32)
            pt[256 * n : 256 * n + 256, at_lane : at_lane + 128] = part.T.astype(BF16)

    transpose_rows(panel.at[0], 0)

    pl.semaphore_wait(barrier, 7 + 16 - own + 8 - own_self + 16 * own - own_self)

    pieces, locs = [], []
    for w in range(WAVES):
        for c in range(2):
            n = 2 * w + c
            piece = remote(
                panel.at[0, c, :, pl.ds((1 - xl) * 512 + w * COLS, COLS)], bufs[w][c].at[g],
                xc_send.at[n], xc_recv.at[n], p, gx,
            )
            piece.start()
            pieces.append(piece)
            loc = pltpu.make_async_copy(
                panel.at[0, c, :, pl.ds(xl * 512 + w * COLS, COLS)], bufs[w][c].at[g], loc_sem.at[n]
            )
            loc.start()
            locs.append(loc)
    misc = [
        remote(anc_v, ancp_v, misc_send.at[0], misc_recv.at[0], p, gx),
        remote(left_own, left_par, misc_send.at[1], misc_recv.at[1], p, gx),
        remote(panel.at[0], prow, misc_send.at[2], misc_recv.at[2], p, gx),
    ]

    def diag_copy(n):
        pole, grid = owner_of(n)
        rows = pl.ds(pl.multiple_of((n // 2) * 8, 8), 8)
        return pole, grid, remote(wd.at[n % 2, rows], dg.at[p], g_send.at[n], g_recv.at[p], pole, grid)

    def diag_start(n, carry):
        pole, grid, copy = diag_copy(n)

        @pl.when(not_me(pole, grid))
        def _():
            copy.start()

        return carry

    def ring(w, c, s, d):
        slot = lax.rem(z + (16 - s if d == 0 else s), 16)
        rows = pl.ds(2 * slot, 2) if s < STEPS - 1 else pl.ds(2 * slot + d, 1)
        ref = bufs[w][c].at[rows]
        return remote(ref, ref, ring_send.at[w, c, d, s], ring_recv.at[w, c, d, s], p, gr if d == 0 else gl)

    sends = []
    for t in range(max(LAG) + STEPS):
        for w in range(WAVES):
            s = t - LAG[w]
            if not 0 <= s < STEPS:
                continue
            for c in range(2):
                if s == 0:
                    locs[2 * w + c].wait()
                    pieces[2 * w + c].wait_recv()
                for d in range(2):
                    if s > 0:
                        ring(w, c, s - 1, d).wait_recv()
                    copy = ring(w, c, s, d)
                    copy.start()
                    sends.append(copy)
        if t == 1:
            for m in misc:
                m.start()
            lax.fori_loop(0, 8, diag_start, 0)
        if t == 4:
            for m in misc:
                m.wait_recv()
            small = pltpu.make_async_copy(ancp_v, ancp_s, small_sem)
            small.start()
            small.wait()
            transpose_rows(prow, 128)

    def product(w, which):
        left = (left_own, left_par)[which]
        ids = (anc_s, ancp_s)[which]
        rows = []
        for k in range(8):
            j = ids[0, k]
            rows.append(jnp.concatenate([bufs[w][0][j], bufs[w][1][j]], axis=1))
        right = jnp.concatenate(rows, axis=0)
        both = jnp.dot(left[...], right, preferred_element_type=F32)
        real = both[64:, COLS:] - both[:64, :COLS]
        imag = -(both[:64, COLS:] + both[64:, :COLS])
        return real, imag

    xsends, xlocs = [], []
    csends = []
    for w in range(WAVES):
        for c in range(2):
            for d in range(2):
                ring(w, c, STEPS - 1, d).wait_recv()
        terms = []
        for which in range(2):
            real, imag = product(w, which)
            dst = (xs, xo)[which]
            dst[w, 0] = real.astype(BF16)
            dst[w, 1] = imag.astype(BF16)
            terms.append(wr * real - wi * imag)
            terms.append(-wr * imag - wi * real)
        place = off.at[0, :, :, pl.ds(xl * 512 + w * COLS, COLS)]
        copy = remote(xo.at[w], place, xo_send.at[w], xo_recv.at[w], p, gx)
        copy.start()
        xsends.append(copy)
        copy = pltpu.make_async_copy(xs.at[w], place, loc_sem.at[w])
        copy.start()
        xlocs.append(copy)
        weighted = jnp.concatenate(terms, axis=0)
        high = weighted.astype(BF16)
        low = (weighted - high.astype(F32)).astype(BF16)
        split = jnp.concatenate([high, low], axis=1)
        for n in range(4):
            two = jnp.dot(pt[256 * n : 256 * n + 256, :], split, preferred_element_type=F32)
            ds[w][4 * n : 4 * n + 4] = (two[:, :COLS] + two[:, COLS:]).reshape(4, 64, COLS)
        copy = remote(
            ds[w].at[:, pl.ds(pl.multiple_of((1 - core) * 32, 32), 32)], rcs[w],
            c_send.at[w], c_recv.at[w], pc, g,
        )
        copy.start()
        csends.append(copy)

    ysends = []
    for w in range(WAVES):
        csends[w].wait_recv()
        es[w][...] = ds[w][:, pl.ds(pl.multiple_of(core * 32, 32), 32)] + rcs[w][...]
        for k in range(1, 4):
            to = lax.rem(y + k, 4)
            copy = remote(
                es[w].at[:, pl.ds(pl.multiple_of(to * 8, 8), 8)], rys[w].at[k - 1],
                y_send.at[w, k - 1], y_recv.at[w, k - 1], to * 4 + xh * 2 + core, g,
            )
            copy.start()
            ysends.append(copy)

    def z_copy(w, to):
        pole, grid = y * 4 + (to // 8) * 2 + core, 2 * to + xl
        me = xh * 16 + z
        return pole, grid, remote(
            fs[w].at[to], rzs[w].at[me], z_send.at[w, to], z_recv.at[w, me], pole, grid
        )

    def z_start(w, to, carry):
        pole, grid, copy = z_copy(w, to)

        @pl.when(not_me(pole, grid))
        def _():
            copy.start()

        return carry

    for w in range(WAVES):
        for k in range(3):
            ysends[3 * w + k].wait_recv()
        fs[w][...] = es[w][:, pl.ds(pl.multiple_of(y * 8, 8), 8)] + rys[w][0] + rys[w][1] + rys[w][2]
        lax.fori_loop(0, 16, functools.partial(z_start, w), 0)

    @pl.when(owner)
    def _():
        def diag_wait(n, total):
            @pl.when(not_me(n, 2 * z + core))
            def _():
                remote(wd.at[0, pl.ds(0, 8)], dg.at[n], g_send.at[0], g_recv.at[n], n, 2 * z + core).wait_recv()

            return total

        lax.fori_loop(0, 16, diag_wait, 0)

        @pl.when(core == xl)
        def _():
            dg[p] = wd[xl, pl.ds(pl.multiple_of(y * 8, 8), 8)]

        total = dg[0]
        for n in range(1, 16):
            total = total + dg[n]

        for w in range(WAVES):
            def z_wait(n, carry):
                pole, grid = source(n)

                @pl.when(not_me(pole, grid))
                def _():
                    remote(fs[w].at[0], rzs[w].at[n], z_send.at[w, 0], z_recv.at[w, n], pole, grid).wait_recv()

                return carry

            lax.fori_loop(0, 32, z_wait, 0)
            rzs[w][xh * 16 + z] = fs[w][z]
            part = rzs[w][0]
            for n in range(1, 32):
                part = part + rzs[w][n]
            res[:, w * COLS : w * COLS + COLS] = total[:, w * COLS : w * COLS + COLS] - part

    me = y * 2 + xl

    def final_copy(n):
        place = dens.at[pl.ds(pl.multiple_of(y * 8, 8), 8), pl.ds(pl.multiple_of(xl * 512, 512), 512)]
        return remote(res, place, n_send.at[n], n_recv.at[me], n, 2 * z + core)

    @pl.when(owner)
    def _():
        def final_start(n, carry):
            @pl.when(not_me(n, 2 * z + core))
            def _():
                final_copy(n).start()

            return carry

        lax.fori_loop(0, 16, final_start, 0)

        @pl.when(core == xl)
        def _():
            place = dens.at[pl.ds(pl.multiple_of(y * 8, 8), 8), pl.ds(pl.multiple_of(xl * 512, 512), 512)]
            copy = pltpu.make_async_copy(res, place, small_sem)
            copy.start()
            copy.wait()

    def final_wait(n, carry):
        pole, grid = owner_of(n)

        @pl.when(not_me(pole, grid))
        def _():
            place = dens.at[pl.ds(pl.multiple_of((n // 2) * 8, 8), 8), pl.ds(pl.multiple_of(lax.rem(n, 2) * 512, 512), 512)]
            remote(res, place, n_send.at[0], n_recv.at[n], pole, grid).wait_recv()

        return carry

    lax.fori_loop(0, 8, final_wait, 0)

    for copy in xsends:
        copy.wait_recv()
    for copy in xlocs:
        copy.wait()
    for copy in sends + pieces + misc + xsends + csends + ysends:
        copy.wait_send()

    def diag_done(n, carry):
        pole, grid, copy = diag_copy(n)

        @pl.when(not_me(pole, grid))
        def _():
            copy.wait_send()

        return carry

    lax.fori_loop(0, 8, diag_done, 0)
    for w in range(WAVES):
        def z_done(to, carry):
            pole, grid, copy = z_copy(w, to)

            @pl.when(not_me(pole, grid))
            def _():
                copy.wait_send()

            return carry

        lax.fori_loop(0, 16, z_done, 0)

    @pl.when(owner)
    def _():
        def final_done(n, carry):
            @pl.when(not_me(n, 2 * z + core))
            def _():
                final_copy(n).wait_send()

            return carry

        lax.fori_loop(0, 16, final_done, 0)


def shards(panel, inverse_blocks, diag_inverse, ancestors, pole_index, weight_table):
    vmem = pl.BlockSpec(memory_space=pltpu.VMEM)
    smem = pl.BlockSpec(memory_space=pltpu.SMEM)
    dma = pltpu.SemaphoreType.DMA
    per_wave = lambda shape, kind: [pltpu.VMEM(shape, kind)] * WAVES
    scratch = [pltpu.VMEM((32, 64, COLS), BF16)] * (2 * WAVES)
    scratch += [
        pltpu.VMEM((128, 512), BF16),
        pltpu.VMEM((128, 512), BF16),
        pltpu.VMEM((1, 8), jnp.int32),
        pltpu.SMEM((1, 8), jnp.int32),
        pltpu.VMEM((2, 64, 1024), BF16),
        pltpu.VMEM((1024, 256), BF16),
        pltpu.VMEM((WAVES, 2, 64, COLS), BF16),
        pltpu.VMEM((WAVES, 2, 64, COLS), BF16),
    ]
    scratch += per_wave((16, 64, COLS), F32)
    scratch += per_wave((16, 32, COLS), F32)
    scratch += per_wave((16, 32, COLS), F32)
    scratch += per_wave((3, 16, 8, COLS), F32)
    scratch += per_wave((16, 8, COLS), F32)
    scratch += per_wave((32, 8, COLS), F32)
    scratch += [
        pltpu.VMEM((2, 32, 512), F32),
        pltpu.VMEM((16, 8, 512), F32),
        pltpu.VMEM((8, 512), F32),
    ]
    scratch += [
        dma((4,)), dma((4,)), dma((4,)), dma((3,)), dma((3,)), dma,
        dma((WAVES, 2, 2, STEPS)), dma((WAVES, 2, 2, STEPS)),
        dma((WAVES,)), dma((WAVES,)), dma((WAVES,)), dma((WAVES,)),
        dma((WAVES, 3)), dma((WAVES, 3)), dma((WAVES, 16)), dma((WAVES, 32)),
        dma((8,)), dma((16,)), dma((16,)), dma((8,)),
    ]
    return pl.pallas_call(
        kernel,
        out_shape=(
            jax.ShapeDtypeStruct(panel.shape, BF16),
            jax.ShapeDtypeStruct((32, 1024), F32),
        ),
        in_specs=[smem, smem, smem, vmem, vmem, vmem, vmem],
        out_specs=(vmem, vmem),
        scratch_shapes=scratch,
        compiler_params=pltpu.CompilerParams(
            collective_id=1, has_side_effects=True, vmem_limit_bytes=40 << 20
        ),
    )(ancestors, pole_index, weight_table, panel, inverse_blocks, diag_inverse, ancestors)


def solution(mesh):
    placed = (
        P("pole", None, "grid", None),
        P("pole", "grid", None, None, None, None),
        P("pole", "grid", None),
        P("grid", None),
        P("pole"),
        P(),
    )
    return jax.shard_map(
        shards,
        mesh=mesh,
        in_specs=placed,
        out_specs=(P("pole", None, "grid", None), P("grid", None)),
        check_vma=False,
    )
```

```python
import jax
import jax.numpy as jnp
from jax import lax
from jax.experimental import pallas as pl
from jax.experimental.pallas import tpu as pltpu
from jax.sharding import PartitionSpec as P

MESH = pl.DeviceIdType.MESH
F32 = jnp.float32
BF16 = jnp.bfloat16
NEAR = (0, 1, 7, 2, 6, 3, 5, 4)


def kernel(
    anc_v, pole_s, table_s, panel_h, inv_h, diag_h,
    off, dens,
    panel, inv, diag, left, wt, pr, lr, buf, lbuf, ancb_v, ancb_s, wtb, prow, xb, yt, d, rx, fb, rz, wd, dg, res,
    in_sem, one_sem,
    p_send, p_recv, l_send, l_recv, pz_send, pz_recv, lz_send, lz_recv, a_send, a_recv, w_send, w_recv,
    xg_send, xg_recv, yg_send, yg_recv, cg_send, cg_recv, cr_send, cr_recv,
    ly_send, ly_recv, lc_send, lc_recv,
    g_send, g_recv, r_send, o_recv, xr_send, xr_recv, z_send, z_recv, n_send, n_recv,
):
    g = lax.axis_index("grid")
    p = lax.axis_index("pole")
    z, xl = g // 2, g % 2
    y, xh, core = p // 4, (p // 2) % 2, p % 2
    u = 2 * y + core
    x = 2 * xh + xl
    half = z // 2
    odd = z % 2
    relay = odd == xh

    def remote(src, dst, send, recv, pole, grid):
        return pltpu.make_async_remote_copy(
            src_ref=src, dst_ref=dst, send_sem=send, recv_sem=recv,
            device_id={"pole": pole, "grid": grid}, device_id_type=MESH,
        )

    def other(pole, grid):
        return jnp.logical_or(pole != p, grid != g)

    def each(count, body):
        def step(n, carry):
            body(n)
            return carry

        lax.fori_loop(0, count, step, 0)

    barrier = pltpu.get_barrier_semaphore()

    def hello(pole, grid):
        @pl.when(other(pole, grid))
        def _():
            pl.semaphore_signal(barrier, inc=1, device_id={"pole": pole, "grid": grid}, device_id_type=MESH)

    each(16, lambda n: hello(p, 2 * n + xl))
    each(32, lambda n: hello(n // 2, 2 * z + n % 2))
    loads = [
        pltpu.make_async_copy(panel_h, panel, in_sem.at[0]),
        pltpu.make_async_copy(inv_h, inv, in_sem.at[1]),
        pltpu.make_async_copy(diag_h, diag, in_sem.at[2]),
    ]
    for load in loads:
        load.start()
    pl.semaphore_wait(barrier, 15 + 31)

    def target(n):
        return (n // 2) * 4 + odd * 2 + n % 2

    def aligned(n, size):
        return pl.ds(pl.multiple_of(n * size, size), size)

    def send_p(n):
        return remote(panel.at[0, :, :, aligned(n, 128)], pr.at[p], p_send.at[n], p_recv.at[p], target(n), g)

    def left_part(n):
        return left.at[aligned(n % 2, 64), aligned(n // 2, 128)]

    def send_l(n):
        return remote(left_part(n), lr.at[p], l_send.at[n], l_recv.at[p], target(n), g)

    def start_first(make):
        def start(n):
            @pl.when(target(n) != p)
            def _():
                make(n).start()

        each(8, start)

    loads[0].wait()
    start_first(send_p)
    own_p = pltpu.make_async_copy(panel.at[0, :, :, aligned(u, 128)], pr.at[p], one_sem.at[0])
    own_p.start()

    loads[1].wait()
    for k in range(0, 8, 2):
        left[:, 64 * k : 64 * k + 128] = jnp.concatenate(
            [inv[0, 0, k].reshape(128, 64), inv[0, 0, k + 1].reshape(128, 64)], axis=1
        )
    start_first(send_l)
    own_l = pltpu.make_async_copy(left_part(u), lr.at[p], one_sem.at[1])
    own_l.start()
    own_p.wait()
    own_l.wait()

    index = pole_s[0]
    my_wr = table_s[index, 0]
    my_wi = table_s[index, 1]
    is_real = lax.broadcasted_iota(jnp.int32, (8, 128), 0) == 0
    wt[...] = jnp.where(is_real, my_wr, my_wi)

    def send_a(q):
        return remote(anc_v, ancb_v.at[half], a_send.at[q], a_recv.at[half], p, 2 * q + xl)

    def send_w(q):
        return remote(wt, wtb, w_send.at[q], w_recv, q, g)

    def start_a(q):
        @pl.when(q != z)
        def _():
            send_a(q).start()

    def start_w(q):
        @pl.when(q != p)
        def _():
            send_w(q).start()

    row = 4 * half + 2 * odd + xl
    l_place = (aligned(core, 64), aligned(y, 128))

    def send_pz(q):
        return remote(pr.at[q], buf.at[row], pz_send.at[q], pz_recv.at[half], p, 2 * q + xl)

    def send_lz(q):
        return remote(lr.at[q], lbuf.at[(half,) + l_place], lz_send.at[q], lz_recv.at[half], p, 2 * q + xl)

    @pl.when(relay)
    def _():
        for far in (8, 7, 9, 6, 10, 5, 11, 4, 12, 3, 13, 2, 14, 1, 15):
            q = lax.rem(z + far, 16)

            @pl.when(q != p)
            def _():
                remote(pr.at[0], pr.at[q], p_send.at[0], p_recv.at[q], q, g).wait_recv()

            send_pz(q).start()

        for far in (8, 7, 9, 6, 10, 5, 11, 4, 12, 3, 13, 2, 14, 1, 15):
            q = lax.rem(z + far, 16)

            @pl.when(q != p)
            def _():
                remote(lr.at[0], lr.at[q], l_send.at[0], l_recv.at[q], q, g).wait_recv()

            send_lz(q).start()

        @pl.when(z != p)
        def _():
            remote(pr.at[0], pr.at[z], p_send.at[0], p_recv.at[z], z, g).wait_recv()
            remote(lr.at[0], lr.at[z], l_send.at[0], l_recv.at[z], z, g).wait_recv()

        buf[row] = pr[z]
        copies = [
            pltpu.make_async_copy(lr.at[z], lbuf.at[(half,) + l_place], one_sem.at[0]),
            pltpu.make_async_copy(anc_v, ancb_v.at[half], one_sem.at[1]),
        ]
        for copy in copies:
            copy.start()
        each(16, start_a)
        for copy in copies:
            copy.wait()

    @pl.when(z == p)
    def _():
        wtb[...] = wt[...]
        each(16, start_w)

    loads[2].wait()
    for n in range(8):
        wd[n] = my_wr * diag[0, :, 128 * n : 128 * n + 128] - my_wi * diag[0, :, 1024 + 128 * n : 1152 + 128 * n]

    def holder(n):
        return (n // 4) * 4 + xl * 2 + (n // 2) % 2, 2 * z + n % 2

    def send_d(n):
        pole, grid = holder(n)
        return remote(wd.at[n // 2, aligned(n % 2, 16)], dg.at[p], g_send.at[n], g_recv.at[p], pole, grid)

    def start_d(n):
        pole, grid = holder(n)

        @pl.when(other(pole, grid))
        def _():
            send_d(n).start()

    each(16, start_d)

    @pl.when(xl == xh)
    def _():
        dg[p] = wd[u, aligned(xl, 16)]

    def at_x(k):
        to = lax.rem(x + k, 4)
        return y * 4 + (to // 2) * 2 + core, 2 * z + to % 2

    def at_y(k):
        return lax.rem(y + k, 4) * 4 + xh * 2 + core

    partner = p + 1 - 2 * core

    def source(m):
        return p, 2 * (2 * m + xh) + xl

    def wait_other(m, make):
        @pl.when(2 * m + xh != z)
        def _():
            make().wait_recv()

    def send_x(k, m):
        block = buf.at[4 * m + x]
        pole, grid = at_x(k)
        return remote(block, block, xg_send.at[k - 1, m], xg_recv.at[k - 1, m], pole, grid)

    def send_y(k, m):
        return remote(
            buf.at[4 * m + x], prow.at[u, m], yg_send.at[k - 1, m], yg_recv.at[k - 1, m], at_y(k), g
        )

    def send_c(m):
        return remote(buf.at[4 * m + x], prow.at[u, m], cg_send.at[m], cg_recv.at[m], partner, g)

    for near in NEAR:
        m = lax.rem(half + near, 8)
        wait_other(m, lambda: remote(pr.at[0], buf.at[4 * m + x], pz_send.at[0], pz_recv.at[m], *source(m)))
        for k in (2, 1, 3):
            send_y(k, m).start()
            send_x(k, m).start()
        send_c(m).start()
        prow[u, m] = buf[4 * m + x]

    own_part = (slice(None), aligned(core, 64), aligned(y, 128))

    def send_ly(k):
        part = lbuf.at[own_part]
        return remote(part, part, ly_send.at[k - 1], ly_recv.at[k - 1], at_y(k), g)

    for near in NEAR:
        m = lax.rem(half + near, 8)
        wait_other(m, lambda: remote(lr.at[0], lbuf.at[(m,) + l_place], lz_send.at[0], lz_recv.at[m], *source(m)))
        wait_other(m, lambda: remote(anc_v, ancb_v.at[m], a_send.at[0], a_recv.at[m], *source(m)))

    @pl.when(z != p)
    def _():
        remote(wt, wtb, w_send.at[0], w_recv, z, g).wait_recv()

    for k in (2, 1, 3):
        send_ly(k).start()
    small = pltpu.make_async_copy(ancb_v, ancb_s, one_sem.at[0])
    small.start()
    small.wait()

    def send_cr(k):
        came = prow.at[2 * lax.rem(y + 4 - k, 4) + core]
        return remote(came, came, cr_send.at[k - 1], cr_recv.at[k - 1], partner, g)

    for k in (1, 3, 2):
        def wait_y(m):
            send_y(k, m).wait_recv()

        each(8, wait_y)
        send_cr(k).start()
    for k in range(1, 4):
        send_ly(k).wait_recv()
    rows_here = lbuf.at[:, aligned(core, 64), :]
    send_lc = remote(rows_here, rows_here, lc_send, lc_recv, partner, g)
    send_lc.start()
    for k in range(1, 4):
        each(8, lambda m: send_x(k, m).wait_recv())
    send_lc.wait_recv()

    wr = wtb[0:1, :]
    wi = wtb[1:2, :]

    off_place = off.at[0, :, :, aligned(u, 128)]

    def send_r(m):
        return remote(xb.at[m], off_place, r_send.at[m], o_recv.at[u], z, 2 * (2 * m + xh) + xl)

    def start_r(m):
        @pl.when(other(z, 2 * (2 * m + xh) + xl))
        def _():
            send_r(m).start()

    for m in range(8):
        rows = []
        for k in range(8):
            j = ancb_s[m, 0, k]
            rows.append(jnp.concatenate([buf[j, 0], buf[j, 1]], axis=1))
        both = jnp.dot(lbuf[m], jnp.concatenate(rows, axis=0), preferred_element_type=F32)
        real = both[64:, 128:] - both[:64, :128]
        imag = -(both[:64, 128:] + both[64:, :128])
        xb[m, 0] = real.astype(BF16)
        xb[m, 1] = imag.astype(BF16)
        start_r(m)
        term = jnp.concatenate([wr * real - wi * imag, -wr * imag - wi * real], axis=0).T
        high = term.astype(BF16)
        yt[0:128, 128 * m : 128 * m + 128] = high
        yt[128:256, 128 * m : 128 * m + 128] = (term - high.astype(F32)).astype(BF16)

    each(8, lambda m: send_c(m).wait_recv())
    for k in range(1, 4):
        send_cr(k).wait_recv()
    for n in range(4):
        columns = jnp.concatenate([prow[2 * n].reshape(1024, 128), prow[2 * n + 1].reshape(1024, 128)], axis=1)
        two = jnp.dot(yt[...], columns, preferred_element_type=F32)
        one = two[:128] + two[128:]
        d[4 * n : 4 * n + 2] = one[:, :128].T.reshape(2, 64, 128)
        d[4 * n + 2 : 4 * n + 4] = one[:, 128:].T.reshape(2, 64, 128)

    def send_xr(k):
        pole, grid = at_x(k)
        return remote(d.at[:, aligned(lax.rem(x + k, 4), 16)], rx.at[k - 1], xr_send.at[k - 1], xr_recv.at[k - 1], pole, grid)

    for k in (2, 1, 3):
        send_xr(k).start()
    for k in range(1, 4):
        send_xr(k).wait_recv()
    fb[...] = d[:, aligned(x, 16)] + rx[0] + rx[1] + rx[2]

    def send_z(k):
        to = lax.rem(z + k, 16)
        return remote(fb.at[to], rz.at[z], z_send.at[k], z_recv.at[z], p, 2 * to + xl)

    each(15, lambda n: send_z(n + 1).start())

    @pl.when(jnp.logical_and(z == p, relay))
    def _():
        home = pltpu.make_async_copy(xb.at[half], off_place, one_sem.at[1])
        home.start()
        home.wait()

    def wait_d(n):
        @pl.when(other(n, 2 * z + xh))
        def _():
            remote(wd.at[0, pl.ds(0, 16)], dg.at[n], g_send.at[0], g_recv.at[n], n, 2 * z + xh).wait_recv()

    each(16, wait_d)
    total = dg[0]
    for n in range(1, 16):
        total = total + dg[n]

    def wait_z(n):
        @pl.when(n != z)
        def _():
            remote(fb.at[0], rz.at[n], z_send.at[0], z_recv.at[n], p, 2 * n + xl).wait_recv()

    each(16, wait_z)
    rz[z] = fb[z]
    part = rz[0]
    for n in range(1, 16):
        part = part + rz[n]
    res[...] = total - part

    place = dens.at[aligned(xl, 16), aligned(u, 128)]
    me = 2 * u + xl

    def send_n(n):
        return remote(res, place, n_send.at[n], n_recv.at[me], n, 2 * z + xh)

    def start_n(n):
        @pl.when(other(n, 2 * z + xh))
        def _():
            send_n(n).start()

    each(16, start_n)

    @pl.when(xl == xh)
    def _():
        copy = pltpu.make_async_copy(res, place, one_sem.at[2])
        copy.start()
        copy.wait()

    def wait_n(n):
        pole, grid = holder(n)

        @pl.when(other(pole, grid))
        def _():
            there = dens.at[aligned(n % 2, 16), aligned(n // 2, 128)]
            remote(res, there, n_send.at[0], n_recv.at[n], pole, grid).wait_recv()

    each(16, wait_n)

    def wait_o(n):
        @pl.when(other(target(n), 2 * p + xl))
        def _():
            remote(xb.at[0], off.at[0, :, :, aligned(n, 128)], r_send.at[0], o_recv.at[n], target(n), 2 * p + xl).wait_recv()

    each(8, wait_o)

    def done_first(n):
        @pl.when(target(n) != p)
        def _():
            send_p(n).wait_send()
            send_l(n).wait_send()

    each(8, done_first)

    @pl.when(relay)
    def _():
        def done_z(q):
            @pl.when(q != z)
            def _():
                send_pz(q).wait_send()
                send_lz(q).wait_send()
                send_a(q).wait_send()

        each(16, done_z)

    @pl.when(z == p)
    def _():
        def done_w(q):
            @pl.when(q != p)
            def _():
                send_w(q).wait_send()

        each(16, done_w)

    def done_d(n):
        pole, grid = holder(n)

        @pl.when(other(pole, grid))
        def _():
            send_d(n).wait_send()

    each(16, done_d)

    def done_m(m):
        for k in range(1, 4):
            send_y(k, m).wait_send()
            send_x(k, m).wait_send()
        send_c(m).wait_send()

        @pl.when(other(z, 2 * (2 * m + xh) + xl))
        def _():
            send_r(m).wait_send()

    each(8, done_m)
    for k in range(1, 4):
        send_ly(k).wait_send()
        send_cr(k).wait_send()
        send_xr(k).wait_send()
    send_lc.wait_send()
    each(15, lambda n: send_z(n + 1).wait_send())

    def done_n(n):
        @pl.when(other(n, 2 * z + xh))
        def _():
            send_n(n).wait_send()

    each(16, done_n)


def shards(panel, inverse_blocks, diag_inverse, ancestors, pole_index, weight_table):
    vmem = pl.BlockSpec(memory_space=pltpu.VMEM)
    smem = pl.BlockSpec(memory_space=pltpu.SMEM)
    hbm = pl.BlockSpec(memory_space=pltpu.HBM)
    dma = pltpu.SemaphoreType.DMA
    scratch = [
        pltpu.VMEM((1, 2, 64, 1024), BF16),
        pltpu.VMEM((1, 1, 8, 2, 64, 64), BF16),
        pltpu.VMEM((1, 32, 2048), F32),
        pltpu.VMEM((128, 512), BF16),
        pltpu.VMEM((8, 128), F32),
        pltpu.VMEM((16, 2, 64, 128), BF16),
        pltpu.VMEM((16, 64, 128), BF16),
        pltpu.VMEM((32, 2, 64, 128), BF16),
        pltpu.VMEM((8, 128, 512), BF16),
        pltpu.VMEM((8, 1, 8), jnp.int32),
        pltpu.SMEM((8, 1, 8), jnp.int32),
        pltpu.VMEM((8, 128), F32),
        pltpu.VMEM((8, 8, 2, 64, 128), BF16),
        pltpu.VMEM((8, 2, 64, 128), BF16),
        pltpu.VMEM((256, 1024), BF16),
        pltpu.VMEM((16, 64, 128), F32),
        pltpu.VMEM((3, 16, 16, 128), F32),
        pltpu.VMEM((16, 16, 128), F32),
        pltpu.VMEM((16, 16, 128), F32),
        pltpu.VMEM((8, 32, 128), F32),
        pltpu.VMEM((16, 16, 128), F32),
        pltpu.VMEM((16, 128), F32),
        dma((3,)), dma((4,)),
        dma((8,)), dma((16,)), dma((8,)), dma((16,)),
        dma((16,)), dma((8,)), dma((16,)), dma((8,)), dma((16,)), dma((8,)), dma((16,)), dma,
        dma((3, 8)), dma((3, 8)), dma((3, 8)), dma((3, 8)), dma((8,)), dma((8,)), dma((3,)), dma((3,)),
        dma((3,)), dma((3,)), dma, dma,
        dma((16,)), dma((16,)), dma((8,)), dma((8,)), dma((3,)), dma((3,)),
        dma((16,)), dma((16,)), dma((16,)), dma((16,)),
    ]
    return pl.pallas_call(
        kernel,
        out_shape=(
            jax.ShapeDtypeStruct(panel.shape, BF16),
            jax.ShapeDtypeStruct((32, 1024), F32),
        ),
        in_specs=[vmem, smem, smem, hbm, hbm, hbm],
        out_specs=(vmem, vmem),
        scratch_shapes=scratch,
        compiler_params=pltpu.CompilerParams(
            collective_id=1, has_side_effects=True, vmem_limit_bytes=32 << 20
        ),
    )(ancestors, pole_index, weight_table, panel, inverse_blocks, diag_inverse)


def solution(mesh):
    placed = (
        P("pole", None, "grid", None),
        P("pole", "grid", None, None, None, None),
        P("pole", "grid", None),
        P("grid", None),
        P("pole"),
        P(),
    )
    return jax.shard_map(
        shards,
        mesh=mesh,
        in_specs=placed,
        out_specs=(P("pole", None, "grid", None), P("grid", None)),
        check_vma=False,
    )
```

```python
import jax
import jax.numpy as jnp
from jax import lax
from jax.experimental import pallas as pl
from jax.experimental.pallas import tpu as pltpu
from jax.sharding import PartitionSpec as P

MESH = pl.DeviceIdType.MESH
F32 = jnp.float32
BF16 = jnp.bfloat16
VMEM = 60 << 20
HOME = ((8, 6, 10, 4, 12, 2, 14, 0), (7, 9, 5, 11, 3, 13, 1, 15))
HELD = 6
DIRECT = 6
FAR = ((8, 4, 12, 0, 6, 10, 2, 14), (7, 9, 1, 15, 5, 11, 3, 13))


def kernel(
    anc_v, pole_s, table_s, panel_h, inv_h, diag_h,
    off, dens,
    panel, inv, diag, left, wt, ar, pr, lr, buf, lbuf, ancb_v, ancb_s, wtb, prow, xb, yt, d, rx, fb, rz, wd, dg, res,
    reach_sem, in_sem, one_sem,
    p_send, p_recv, l_send, l_recv, h_send, h_recv, pz_send, pz_recv, lz_send, lz_recv, a_send, a_recv, w_send, w_recv,
    xg_send, xg_recv, yg_send, yg_recv, cg_send, cg_recv, cr_send, cr_recv,
    ly_send, ly_recv, lc_send, lc_recv,
    g_send, g_recv, r_send, o_recv, xr_send, xr_recv, z_send, z_recv, n_send, n_recv,
):
    g = lax.axis_index("grid")
    p = lax.axis_index("pole")
    z, xl = g // 2, g % 2
    y, xh, core = p // 4, (p // 2) % 2, p % 2
    u = 2 * y + core
    x = 2 * xh + xl
    half = z // 2
    odd = z % 2
    own_parity = 1 - lax.rem(xh + xl, 2)
    part = lax.rem(x + 3 + 2 * odd, 4)
    parity = part // 2
    pole_core = lax.rem(z + own_parity, 2)
    passed_part = 2 * odd + 1 - xl
    partner = p + 1 - 2 * core
    gx = g + 1 - 2 * xl

    def remote(src, dst, send, recv, pole, grid):
        return pltpu.make_async_remote_copy(
            src_ref=src, dst_ref=dst, send_sem=send, recv_sem=recv,
            device_id={"pole": pole, "grid": grid}, device_id_type=MESH,
        )

    def wait_in(ref, sem):
        remote(ref, ref, sem, sem, partner, g).wait_recv()

    def wait_out(ref, sem):
        remote(ref, ref, sem, sem, partner, g).wait_send()

    def other(pole, grid):
        return jnp.logical_or(pole != p, grid != g)

    def each(count, body):
        def step(n, carry):
            body(n)
            return carry

        lax.fori_loop(0, count, step, 0)

    def aligned(n, size):
        return pl.ds(pl.multiple_of(n * size, size), size)

    barrier = pltpu.get_barrier_semaphore()

    def hello(pole, grid):
        @pl.when(other(pole, grid))
        def _():
            pl.semaphore_signal(barrier, inc=1, device_id={"pole": pole, "grid": grid}, device_id_type=MESH)

    loads = [
        pltpu.make_async_copy(inv_h, inv, in_sem.at[0]),
        pltpu.make_async_copy(panel_h, panel, in_sem.at[1]),
        pltpu.make_async_copy(diag_h, diag, in_sem.at[2]),
    ]
    for load in loads:
        load.start()
    next_z, last_z = [2 * lax.rem(z + k, 16) + xl for k in (1, 15)]
    hello(p, next_z)
    hello(p, last_z)
    each(32, lambda n: hello(n // 2, 2 * z + n % 2))
    loads[0].wait()
    for k in range(0, 8, 2):
        left[:, 64 * k : 64 * k + 128] = jnp.concatenate(
            [inv[0, 0, k].reshape(128, 64), inv[0, 0, k + 1].reshape(128, 64)], axis=1
        )
    loads[1].wait()
    pl.semaphore_wait(barrier, 2 + 31)

    def reach(n):
        for k in (1 << n, 16 - (1 << n)):
            pl.semaphore_signal(
                reach_sem.at[n], inc=1,
                device_id={"pole": p, "grid": 2 * lax.rem(z + k, 16) + xl}, device_id_type=MESH,
            )

    reach(0)

    def target(n):
        return (n // 2) * 4 + lax.rem(xl + odd + core, 2) * 2 + n % 2

    def send_l(k):
        n = lax.rem(u + k, 8)
        piece = left.at[aligned(n % 2, 64), aligned(n // 2, 128)]
        remote(piece, lr.at[p // 2], l_send, l_recv.at[p // 2], target(n), gx).start()

    def send_p(k):
        n = lax.rem(u + k, 8)
        remote(panel.at[0, :, :, aligned(n, 128)], pr.at[p // 2], p_send, p_recv.at[p // 2], target(n), gx).start()

    @pl.when(xh == 0)
    def _():
        for n in range(2):
            remote(anc_v, ar, h_send.at[n], h_recv, target(2 * y + n), gx).start()

    each(8, send_l)
    each(8, send_p)
    for n in range(3):
        pl.semaphore_wait(reach_sem.at[n], 2)
        if n < 2:
            reach(n + 1)

    index = pole_s[0]
    my_wr = table_s[0, index]
    my_wi = table_s[1, index]
    is_real = lax.broadcasted_iota(jnp.int32, (8, 128), 0) == 0
    wt[...] = jnp.where(is_real, my_wr, my_wi)

    @pl.when(z == p)
    def _():
        def send_w(q):
            @pl.when(q != p)
            def _():
                remote(wt, wtb, w_send.at[q], w_recv, q, g).start()

        wtb[...] = wt[...]
        each(16, send_w)

    l_place = (aligned(core, 64), aligned(y, 128))

    def pole_of(n):
        from_u = lax.rem(u + 8 - 2 * (n // 2) - lax.rem(core + pole_core, 2), 8)
        return (from_u // 2) * 4 + (n % 2) * 2 + pole_core

    def pole_far(n):
        return lax.rem(z + jnp.where(own_parity == 0, FAR[0][n], FAR[1][n]), 16)

    def pass_l(n):
        q = pole_of(n)
        ref = lr.at[q // 2]
        wait_in(ref, l_recv.at[q // 2])

        @pl.when(q != z)
        def _():
            remote(ref, lbuf.at[(half,) + l_place], lz_send, lz_recv.at[half], p, 2 * q + xl).start()

    def pass_p(n):
        q = pole_far(n)
        ref = pr.at[q // 2]
        wait_in(ref, p_recv.at[q // 2])

        @pl.when(q != z)
        def _():
            remote(ref, buf.at[half, passed_part], pz_send.at[n // 4], pz_recv.at[half], p, 2 * q + xl).start()

    def pass_a(n):
        q = 2 * n + pole_core

        @pl.when(q != z)
        def _():
            remote(ar, ancb_v.at[half], a_send.at[n], a_recv.at[half], p, 2 * q + xl).start()

    def sent(ref, sem, count):
        @pl.when(own_parity == 0)
        def _():
            wait_out(ref.at[0 : count - 1], sem)

        @pl.when(own_parity != 0)
        def _():
            wait_out(ref.at[0:count], sem)

    each(8, pass_l)
    sent(lr, lz_send, 8)
    for n in range(4):
        pass_p(n)
    wait_in(ar, h_recv)
    each(8, pass_a)

    @pl.when(own_parity == 0)
    def _():
        copies = [
            pltpu.make_async_copy(lr.at[half], lbuf.at[(half,) + l_place], one_sem.at[1]),
            pltpu.make_async_copy(ar, ancb_v.at[half], one_sem.at[2]),
        ]
        for copy in copies:
            copy.start()
        for copy in copies:
            copy.wait()

    loads[2].wait()
    for n in range(8):
        wd[n] = my_wr * diag[0, :, 128 * n : 128 * n + 128] - my_wi * diag[0, :, 1024 + 128 * n : 1152 + 128 * n]

    def holder(n):
        return (n // 4) * 4 + xl * 2 + (n // 2) % 2, 2 * z + n % 2

    def send_d(n):
        pole, grid = holder(n)

        @pl.when(other(pole, grid))
        def _():
            remote(wd.at[n // 2, aligned(n % 2, 16)], dg.at[p], g_send, g_recv, pole, grid).start()

    each(16, send_d)

    @pl.when(xl == xh)
    def _():
        dg[p] = wd[u, aligned(xl, 16)]

    def at_x(k):
        to = lax.rem(x + k, 4)
        return y * 4 + (to // 2) * 2 + core, 2 * z + to % 2

    def at_y(k):
        return lax.rem(y + k, 4) * 4 + xh * 2 + core

    def from_z(m, ref, sem):
        @pl.when(2 * m + parity != z)
        def _():
            wait_in(ref, sem.at[m])

    for m in range(8):
        from_z(m, lbuf.at[(m,) + l_place], lz_recv)

    def l_of(k, rows):
        return lbuf.at[rows, aligned(core, 64), aligned(lax.rem(y + k, 4), 128)]

    whole = slice(0, 8)
    for k, n in ((1, 0), (3, 1)):
        ref = l_of(0, whole)
        remote(ref, ref, ly_send.at[0], ly_recv.at[n], at_y(k), g).start()
    sent(pr, pz_send.at[0], 4)
    for n in range(4, 8):
        pass_p(n)

    @pl.when(own_parity == 0)
    def _():
        copy = pltpu.make_async_copy(pr.at[half], buf.at[half, part], one_sem.at[0])
        copy.start()
        copy.wait()

    for k, n, to, rows in ((3, 0, 1, slice(0, 4)), (1, 1, 3, slice(4, 8))):
        wait_in(l_of(k, whole), ly_recv.at[n])
        ref = l_of(k, rows)
        remote(ref, ref, ly_send.at[1], ly_recv.at[2 + n], at_y(to), g).start()
    for m in range(8):
        from_z(m, ancb_v.at[m], a_recv)
    small = pltpu.make_async_copy(ancb_v, ancb_s, one_sem.at[0])
    small.start()

    def far_m(own, i):
        return lax.rem(z + 16 - jnp.where(own == 0, FAR[0][i], FAR[1][i]), 16) // 2

    def x_part(k):
        return lax.rem(part + k, 4)

    def x_own(k):
        to = lax.rem(x + k, 4)
        return 1 - lax.rem(to // 2 + to % 2, 2)

    def y_part(k):
        return 2 * lax.rem(y + k, 4) + core

    ways = ((1, 0), (3, 1))
    rows_here = lbuf.at[:, aligned(core, 64), :]

    def start_one(i):
        m = far_m(own_parity, i)
        block = buf.at[m, part]
        there = prow.at[u, m]
        for k, n in ways + (((2, 2),) if i >= DIRECT else ()):
            pole, grid = at_x(k)
            remote(block, block, xg_send, xg_recv.at[n, i], pole, grid).start()
            remote(block, there, yg_send, yg_recv.at[n, i], at_y(k), g).start()
        remote(block, there, cg_send, cg_recv, partner, g).start()
        prow[u, m] = buf[m, part]

    def pass_one(i):
        m = far_m(own_parity, i)
        for k, n in ((3, 0), (1, 1)):
            ref = buf.at[far_m(x_own(k), i), x_part(k)]
            wait_in(ref, xg_recv.at[n, i])
            if i < DIRECT and i % 2 == n:
                pole, grid = at_x(4 - k)
                remote(ref, ref, xg_send, xg_recv.at[2, i], pole, grid).start()
        for k, n in ((3, 0), (1, 1)):
            ref = prow.at[y_part(k), m]
            wait_in(ref, yg_recv.at[n, i])
            if i < DIRECT and i % 2 == n:
                remote(ref, ref, yg_send, yg_recv.at[2, i], at_y(4 - k), g).start()

    def arrived(i):
        from_z(far_m(own_parity, i), buf.at[far_m(own_parity, i), part], pz_recv)

    for i in range(4):
        arrived(i)
        start_one(i)
    for n, rows in ((0, slice(0, 4)), (1, slice(4, 8))):
        wait_in(l_of(2, rows), ly_recv.at[2 + n])
    remote(rows_here, rows_here, lc_send, lc_recv, partner, g).start()
    for i in range(4):
        pass_one(i)
    for i in range(4, 8):
        arrived(i)
        start_one(i)
    for i in range(4, 8):
        pass_one(i)

    def send_cr(k):
        came = prow.at[y_part(k)]
        remote(came, came, cr_send, cr_recv, partner, g).start()

    send_cr(3)
    send_cr(1)
    for i in range(8):
        wait_in(buf.at[far_m(x_own(2), i), x_part(2)], xg_recv.at[2, i])
    for i in range(8):
        wait_in(prow.at[y_part(2), far_m(own_parity, i)], yg_recv.at[2, i])
    send_cr(2)
    small.wait()
    wait_in(rows_here, lc_recv)

    @pl.when(z != p)
    def _():
        wait_in(wtb, w_recv)

    wr = wtb[0:1, :]
    wi = wtb[1:2, :]
    off_place = off.at[0, :, :, aligned(u, 128)]

    def send_home(i):
        m = lax.rem(z + 16 - jnp.where(own_parity == 0, HOME[0][i], HOME[1][i]), 16) // 2
        remote(xb.at[m], off_place, r_send, o_recv, z, 2 * (2 * m + parity) + 1 - xl).start()

    for m in range(8):
        rows = []
        for k in range(8):
            j = ancb_s[m, 0, k]
            rows.append(jnp.concatenate([buf[j // 4, j % 4, 0], buf[j // 4, j % 4, 1]], axis=1))
        both = jnp.dot(lbuf[m], jnp.concatenate(rows, axis=0), preferred_element_type=F32)
        real = both[64:, 128:] - both[:64, :128]
        imag = -(both[:64, 128:] + both[64:, :128])
        xb[m, 0] = real.astype(BF16)
        xb[m, 1] = imag.astype(BF16)
        term = jnp.concatenate([wr * real - wi * imag, -wr * imag - wi * real], axis=0).T
        high = term.astype(BF16)
        yt[0:128, 128 * m : 128 * m + 128] = high
        yt[128:256, 128 * m : 128 * m + 128] = (term - high.astype(F32)).astype(BF16)

    for i in range(HELD):
        send_home(i)
    wait_in(prow.at[0], cg_recv)
    wait_in(prow.at[0:3], cr_recv)
    for n in range(4):
        columns = jnp.concatenate([prow[2 * n].reshape(1024, 128), prow[2 * n + 1].reshape(1024, 128)], axis=1)
        two = jnp.dot(yt[...], columns, preferred_element_type=F32)
        one = two[:128] + two[128:]
        d[4 * n : 4 * n + 2] = one[:, :128].T.reshape(2, 64, 128)
        d[4 * n + 2 : 4 * n + 4] = one[:, 128:].T.reshape(2, 64, 128)

    for h in range(2):
        for k in (2, 1, 3):
            pole, grid = at_x(k)
            there = pl.ds(pl.multiple_of(lax.rem(x + k, 4) * 16 + 8 * h, 8), 8)
            remote(d.at[:, there], rx.at[h, k - 1], xr_send, xr_recv.at[h], pole, grid).start()

    for h in range(2):
        wait_in(rx.at[h], xr_recv.at[h])
        here = pl.ds(pl.multiple_of(x * 16 + 8 * h, 8), 8)
        fb[h] = d[:, here] + rx[h, 0] + rx[h, 1] + rx[h, 2]

        def send_z(n):
            to = lax.rem(z + jnp.where(n % 2 == 0, 8 + n // 2, 7 - n // 2), 16)
            remote(fb.at[h, to], rz.at[h, z], z_send.at[h], z_recv.at[h], p, 2 * to + xl).start()

        each(15, send_z)
    for i in range(HELD, 8):
        send_home(i)

    @pl.when(xl == xh)
    def _():
        wait_in(dg.at[0:15], g_recv)

    @pl.when(xl != xh)
    def _():
        wait_in(dg, g_recv)

    total = dg[0]
    for n in range(1, 16):
        total = total + dg[n]
    for h in range(2):
        rz[h, z] = fb[h, z]
        wait_in(rz.at[h, 0:15], z_recv.at[h])
        minus = rz[h, 0]
        for n in range(1, 16):
            minus = minus + rz[h, n]
        res[8 * h : 8 * h + 8] = total[8 * h : 8 * h + 8] - minus

    place = dens.at[aligned(xl, 16), aligned(u, 128)]

    def send_n(k):
        n = lax.rem(p + k, 16)

        @pl.when(other(n, 2 * z + xh))
        def _():
            remote(res, place, n_send, n_recv, n, 2 * z + xh).start()

    each(16, send_n)

    @pl.when(xl == xh)
    def _():
        copy = pltpu.make_async_copy(res, place, one_sem.at[2])
        copy.start()
        copy.wait()

    wait_out(left, l_send)
    wait_out(panel, p_send)

    @pl.when(xh == 0)
    def _():
        for n in range(2):
            wait_out(ar, h_send.at[n])

    @pl.when(z == p)
    def _():
        def done_w(q):
            @pl.when(q != p)
            def _():
                wait_out(wt, w_send.at[q])

        each(16, done_w)

    def done_a(n):
        @pl.when(2 * n + pole_core != z)
        def _():
            wait_out(ar, a_send.at[n])

    each(8, done_a)

    wait_out(pr.at[0:4], pz_send.at[1])
    wait_out(lbuf.at[:, 0:64, 0:256], ly_send.at[0])
    wait_out(lbuf.at[:, 0:64, 0:128], ly_send.at[1])
    wait_out(rows_here, lc_send)
    wait_out(prow.at[0:3], xg_send)
    wait_out(prow.at[0:3], yg_send)
    wait_out(prow.at[0], cg_send)
    wait_out(prow.at[0:3], cr_send)
    wait_out(xb, r_send)
    wait_out(rx, xr_send)
    for h in range(2):
        wait_out(fb.at[h, 0:15], z_send.at[h])

    @pl.when(xl == xh)
    def _():
        wait_out(dg.at[0:15], g_send)
        wait_out(dg.at[0:15], n_send)
        wait_in(dg.at[0:15], n_recv)

    @pl.when(xl != xh)
    def _():
        wait_out(dg, g_send)
        wait_out(dg, n_send)
        wait_in(dg, n_recv)

    wait_in(xb, o_recv)


def shards(panel, inverse_blocks, diag_inverse, ancestors, pole_index, weight_table):
    vmem = pl.BlockSpec(memory_space=pltpu.VMEM)
    smem = pl.BlockSpec(memory_space=pltpu.SMEM)
    hbm = pl.BlockSpec(memory_space=pl.ANY)
    dma = pltpu.SemaphoreType.DMA
    scratch = [
        pltpu.VMEM((1, 2, 64, 1024), BF16),
        pltpu.VMEM((1, 1, 8, 2, 64, 64), BF16),
        pltpu.VMEM((1, 32, 2048), F32),
        pltpu.VMEM((128, 512), BF16),
        pltpu.VMEM((8, 128), F32),
        pltpu.VMEM((1, 8), jnp.int32),
        pltpu.VMEM((8, 2, 64, 128), BF16),
        pltpu.VMEM((8, 64, 128), BF16),
        pltpu.VMEM((8, 4, 2, 64, 128), BF16),
        pltpu.VMEM((8, 128, 512), BF16),
        pltpu.VMEM((8, 1, 8), jnp.int32),
        pltpu.SMEM((8, 1, 8), jnp.int32),
        pltpu.VMEM((8, 128), F32),
        pltpu.VMEM((8, 8, 2, 64, 128), BF16),
        pltpu.VMEM((8, 2, 64, 128), BF16),
        pltpu.VMEM((256, 1024), BF16),
        pltpu.VMEM((16, 64, 128), F32),
        pltpu.VMEM((2, 3, 16, 8, 128), F32),
        pltpu.VMEM((2, 16, 8, 128), F32),
        pltpu.VMEM((2, 16, 8, 128), F32),
        pltpu.VMEM((8, 32, 128), F32),
        pltpu.VMEM((16, 16, 128), F32),
        pltpu.VMEM((16, 128), F32),
        pltpu.SemaphoreType.REGULAR((3,)), dma((3,)), dma((3,)),
        dma, dma((8,)), dma, dma((8,)), dma((2,)), dma, dma((2,)), dma((8,)), dma, dma((8,)), dma((8,)), dma((8,)), dma((16,)), dma,
        dma, dma((3, 8)), dma, dma((3, 8)), dma, dma, dma, dma,
        dma((2,)), dma((4,)), dma, dma,
        dma, dma, dma, dma, dma, dma((2,)), dma((2,)), dma((2,)), dma, dma,
    ]
    return pl.pallas_call(
        kernel,
        out_shape=(
            jax.ShapeDtypeStruct(panel.shape, BF16),
            jax.ShapeDtypeStruct((32, 1024), F32),
        ),
        in_specs=[vmem, smem, smem, hbm, hbm, hbm],
        out_specs=(hbm, hbm),
        scratch_shapes=scratch,
        compiler_params=pltpu.CompilerParams(
            collective_id=1, has_side_effects=True, vmem_limit_bytes=VMEM
        ),
    )(ancestors, pole_index, weight_table.T, panel, inverse_blocks, diag_inverse)


def solution(mesh):
    placed = (
        P("pole", None, "grid", None),
        P("pole", "grid", None, None, None, None),
        P("pole", "grid", None),
        P("grid", None),
        P("pole"),
        P(),
    )
    return jax.shard_map(
        shards,
        mesh=mesh,
        in_specs=placed,
        out_specs=(P("pole", None, "grid", None), P("grid", None)),
        check_vma=False,
    )
```

```python
import jax
import jax.numpy as jnp
from jax import lax
from jax.experimental import pallas as pl
from jax.experimental.pallas import tpu as pltpu
from jax.sharding import PartitionSpec as P

MESH = pl.DeviceIdType.MESH
F32 = jnp.float32
BF16 = jnp.bfloat16
VMEM = 60 << 20
HOME = ((8, 6, 10, 4, 12, 2, 14, 0), (7, 9, 5, 11, 3, 13, 1, 15))
HELD = 5
DIRECT = 5
FAR = ((8, 4, 12, 0, 6, 10, 2, 14), (7, 9, 1, 15, 5, 11, 3, 13))


def kernel(
    anc_v, pole_s, table_s, panel_h, inv_h, diag_h,
    off, dens,
    panel, inv, diag, left, wt, ar, pr, lr, buf, lbuf, ancb_v, ancb_s, wtb, prow, xb, yt, d, rx, fb, rz, wd, dg, res,
    reach_sem, in_sem, one_sem,
    p_send, p_recv, l_send, l_recv, h_send, h_recv, pz_send, pz_recv, lz_send, lz_recv, a_send, a_recv, w_send, w_recv,
    xg_send, xg_recv, yg_send, yg_recv, cg_send, cg_recv, cr_send, cr_recv,
    ly_send, ly_recv, lc_send, lc_recv,
    g_send, g_recv, r_send, o_recv, xr_send, xr_recv, z_send, z_recv, n_send, n_recv,
):
    g = lax.axis_index("grid")
    p = lax.axis_index("pole")
    z, xl = g // 2, g % 2
    y, xh, core = p // 4, (p // 2) % 2, p % 2
    u = 2 * y + core
    x = 2 * xh + xl
    half = z // 2
    odd = z % 2
    own_parity = 1 - lax.rem(xh + xl, 2)
    part = lax.rem(x + 3 + 2 * odd, 4)
    parity = part // 2
    pole_core = lax.rem(z + own_parity, 2)
    passed_part = 2 * odd + 1 - xl
    partner = p + 1 - 2 * core
    gx = g + 1 - 2 * xl

    def remote(src, dst, send, recv, pole, grid):
        return pltpu.make_async_remote_copy(
            src_ref=src, dst_ref=dst, send_sem=send, recv_sem=recv,
            device_id={"pole": pole, "grid": grid}, device_id_type=MESH,
        )

    def wait_in(ref, sem):
        remote(ref, ref, sem, sem, partner, g).wait_recv()

    def wait_out(ref, sem):
        remote(ref, ref, sem, sem, partner, g).wait_send()

    def other(pole, grid):
        return jnp.logical_or(pole != p, grid != g)

    def each(count, body):
        def step(n, carry):
            body(n)
            return carry

        lax.fori_loop(0, count, step, 0)

    def aligned(n, size):
        return pl.ds(pl.multiple_of(n * size, size), size)

    barrier = pltpu.get_barrier_semaphore()

    def hello(pole, grid):
        @pl.when(other(pole, grid))
        def _():
            pl.semaphore_signal(barrier, inc=1, device_id={"pole": pole, "grid": grid}, device_id_type=MESH)

    loads = [
        pltpu.make_async_copy(inv_h, inv, in_sem.at[0]),
        pltpu.make_async_copy(panel_h, panel, in_sem.at[1]),
        pltpu.make_async_copy(diag_h, diag, in_sem.at[2]),
    ]
    for load in loads:
        load.start()
    next_z, last_z = [2 * lax.rem(z + k, 16) + xl for k in (1, 15)]
    hello(p, next_z)
    hello(p, last_z)
    each(32, lambda n: hello(n // 2, 2 * z + n % 2))
    loads[0].wait()
    for k in range(0, 8, 2):
        left[:, 64 * k : 64 * k + 128] = jnp.concatenate(
            [inv[0, 0, k].reshape(128, 64), inv[0, 0, k + 1].reshape(128, 64)], axis=1
        )
    loads[1].wait()
    pl.semaphore_wait(barrier, 2 + 31)

    def reach(n):
        for k in (1 << n, 16 - (1 << n)):
            pl.semaphore_signal(
                reach_sem.at[n], inc=1,
                device_id={"pole": p, "grid": 2 * lax.rem(z + k, 16) + xl}, device_id_type=MESH,
            )

    reach(0)

    def target(n):
        return (n // 2) * 4 + lax.rem(xl + odd + core, 2) * 2 + n % 2

    def send_l(k):
        n = lax.rem(u + k, 8)
        piece = left.at[aligned(n % 2, 64), aligned(n // 2, 128)]
        remote(piece, lr.at[p // 2], l_send, l_recv.at[p // 2], target(n), gx).start()

    def send_p(k):
        n = lax.rem(u + k, 8)
        remote(panel.at[0, :, :, aligned(n, 128)], pr.at[p // 2], p_send, p_recv.at[p // 2], target(n), gx).start()

    @pl.when(xh == 0)
    def _():
        for n in range(2):
            remote(anc_v, ar, h_send.at[n], h_recv, target(2 * y + n), gx).start()

    each(8, send_l)
    each(8, send_p)
    for n in range(3):
        pl.semaphore_wait(reach_sem.at[n], 2)
        if n < 2:
            reach(n + 1)

    index = pole_s[0]
    my_wr = table_s[0, index]
    my_wi = table_s[1, index]
    is_real = lax.broadcasted_iota(jnp.int32, (8, 128), 0) == 0
    wt[...] = jnp.where(is_real, my_wr, my_wi)

    @pl.when(z == p)
    def _():
        def send_w(q):
            @pl.when(q != p)
            def _():
                remote(wt, wtb, w_send.at[q], w_recv, q, g).start()

        wtb[...] = wt[...]
        each(16, send_w)

    l_place = (aligned(core, 64), aligned(y, 128))

    def pole_of(n):
        from_u = lax.rem(u + 8 - 2 * (n // 2) - lax.rem(core + pole_core, 2), 8)
        return (from_u // 2) * 4 + (n % 2) * 2 + pole_core

    def pole_far(n):
        return lax.rem(z + jnp.where(own_parity == 0, FAR[0][n], FAR[1][n]), 16)

    def pass_l(n):
        q = pole_of(n)
        ref = lr.at[q // 2]
        wait_in(ref, l_recv.at[q // 2])

        @pl.when(q != z)
        def _():
            remote(ref, lbuf.at[(half,) + l_place], lz_send, lz_recv.at[half], p, 2 * q + xl).start()

    def pass_p(n):
        q = pole_far(n)
        ref = pr.at[q // 2]
        wait_in(ref, p_recv.at[q // 2])

        @pl.when(q != z)
        def _():
            remote(ref, buf.at[half, passed_part], pz_send.at[n // 4], pz_recv.at[half], p, 2 * q + xl).start()

    def pass_a(n):
        q = 2 * n + pole_core

        @pl.when(q != z)
        def _():
            remote(ar, ancb_v.at[half], a_send.at[n], a_recv.at[half], p, 2 * q + xl).start()

    def sent(ref, sem, count):
        @pl.when(own_parity == 0)
        def _():
            wait_out(ref.at[0 : count - 1], sem)

        @pl.when(own_parity != 0)
        def _():
            wait_out(ref.at[0:count], sem)

    each(8, pass_l)
    sent(lr, lz_send, 8)
    for n in range(4):
        pass_p(n)
    wait_in(ar, h_recv)
    each(8, pass_a)

    @pl.when(own_parity == 0)
    def _():
        copies = [
            pltpu.make_async_copy(lr.at[half], lbuf.at[(half,) + l_place], one_sem.at[1]),
            pltpu.make_async_copy(ar, ancb_v.at[half], one_sem.at[2]),
        ]
        for copy in copies:
            copy.start()
        for copy in copies:
            copy.wait()

    loads[2].wait()
    for n in range(8):
        wd[n] = my_wr * diag[0, :, 128 * n : 128 * n + 128] - my_wi * diag[0, :, 1024 + 128 * n : 1152 + 128 * n]

    def holder(n):
        return (n // 4) * 4 + xl * 2 + (n // 2) % 2, 2 * z + n % 2

    def send_d(n):
        pole, grid = holder(n)

        @pl.when(other(pole, grid))
        def _():
            remote(wd.at[n // 2, aligned(n % 2, 16)], dg.at[p], g_send, g_recv, pole, grid).start()

    each(16, send_d)

    @pl.when(xl == xh)
    def _():
        dg[p] = wd[u, aligned(xl, 16)]

    def at_x(k):
        to = lax.rem(x + k, 4)
        return y * 4 + (to // 2) * 2 + core, 2 * z + to % 2

    def at_y(k):
        return lax.rem(y + k, 4) * 4 + xh * 2 + core

    def from_z(m, ref, sem):
        @pl.when(2 * m + parity != z)
        def _():
            wait_in(ref, sem.at[m])

    for m in range(8):
        from_z(m, lbuf.at[(m,) + l_place], lz_recv)

    def l_of(k, rows):
        return lbuf.at[rows, aligned(core, 64), aligned(lax.rem(y + k, 4), 128)]

    whole = slice(0, 8)
    for k, n in ((1, 0), (3, 1)):
        ref = l_of(0, whole)
        remote(ref, ref, ly_send.at[0], ly_recv.at[n], at_y(k), g).start()
    sent(pr, pz_send.at[0], 4)
    for n in range(4, 8):
        pass_p(n)

    @pl.when(own_parity == 0)
    def _():
        copy = pltpu.make_async_copy(pr.at[half], buf.at[half, part], one_sem.at[0])
        copy.start()
        copy.wait()

    for k, n, to, rows in ((3, 0, 1, slice(0, 4)), (1, 1, 3, slice(4, 8))):
        wait_in(l_of(k, whole), ly_recv.at[n])
        ref = l_of(k, rows)
        remote(ref, ref, ly_send.at[1], ly_recv.at[2 + n], at_y(to), g).start()
    for m in range(8):
        from_z(m, ancb_v.at[m], a_recv)
    small = pltpu.make_async_copy(ancb_v, ancb_s, one_sem.at[0])
    small.start()

    def far_m(own, i):
        return lax.rem(z + 16 - jnp.where(own == 0, FAR[0][i], FAR[1][i]), 16) // 2

    def x_part(k):
        return lax.rem(part + k, 4)

    def x_own(k):
        to = lax.rem(x + k, 4)
        return 1 - lax.rem(to // 2 + to % 2, 2)

    def y_part(k):
        return 2 * lax.rem(y + k, 4) + core

    ways = ((1, 0), (3, 1))
    rows_here = lbuf.at[:, aligned(core, 64), :]

    def start_one(i):
        m = far_m(own_parity, i)
        block = buf.at[m, part]
        there = prow.at[u, m]
        for k, n in ways + (((2, 2),) if i >= DIRECT else ()):
            pole, grid = at_x(k)
            remote(block, block, xg_send, xg_recv.at[n, i], pole, grid).start()
            remote(block, there, yg_send, yg_recv.at[n, i], at_y(k), g).start()
        remote(block, there, cg_send, cg_recv, partner, g).start()
        prow[u, m] = buf[m, part]

    def pass_one(i):
        m = far_m(own_parity, i)
        for k, n in ((3, 0), (1, 1)):
            ref = buf.at[far_m(x_own(k), i), x_part(k)]
            wait_in(ref, xg_recv.at[n, i])
            if i < DIRECT and i % 2 == n:
                pole, grid = at_x(4 - k)
                remote(ref, ref, xg_send, xg_recv.at[2, i], pole, grid).start()
        for k, n in ((3, 0), (1, 1)):
            ref = prow.at[y_part(k), m]
            wait_in(ref, yg_recv.at[n, i])
            if i < DIRECT and i % 2 == n:
                remote(ref, ref, yg_send, yg_recv.at[2, i], at_y(4 - k), g).start()

    def arrived(i):
        from_z(far_m(own_parity, i), buf.at[far_m(own_parity, i), part], pz_recv)

    for i in range(4):
        arrived(i)
        start_one(i)
    for n, rows in ((0, slice(0, 4)), (1, slice(4, 8))):
        wait_in(l_of(2, rows), ly_recv.at[2 + n])
    remote(rows_here, rows_here, lc_send, lc_recv, partner, g).start()
    for i in range(4, 8):
        pass_one(i - 4)
        arrived(i)
        start_one(i)
    for i in range(4, 8):
        pass_one(i)

    def send_cr(k):
        came = prow.at[y_part(k)]
        remote(came, came, cr_send, cr_recv, partner, g).start()

    send_cr(3)
    send_cr(1)
    for i in range(8):
        wait_in(buf.at[far_m(x_own(2), i), x_part(2)], xg_recv.at[2, i])
    for i in range(8):
        wait_in(prow.at[y_part(2), far_m(own_parity, i)], yg_recv.at[2, i])
    send_cr(2)
    small.wait()
    wait_in(rows_here, lc_recv)

    @pl.when(z != p)
    def _():
        wait_in(wtb, w_recv)

    wr = wtb[0:1, :]
    wi = wtb[1:2, :]
    off_place = off.at[0, :, :, aligned(u, 128)]

    def send_home(i):
        m = lax.rem(z + 16 - jnp.where(own_parity == 0, HOME[0][i], HOME[1][i]), 16) // 2
        remote(xb.at[m], off_place, r_send, o_recv, z, 2 * (2 * m + parity) + 1 - xl).start()

    for m in range(8):
        rows = []
        for k in range(8):
            j = ancb_s[m, 0, k]
            rows.append(jnp.concatenate([buf[j // 4, j % 4, 0], buf[j // 4, j % 4, 1]], axis=1))
        both = jnp.dot(lbuf[m], jnp.concatenate(rows, axis=0), preferred_element_type=F32)
        real = both[64:, 128:] - both[:64, :128]
        imag = -(both[:64, 128:] + both[64:, :128])
        xb[m, 0] = real.astype(BF16)
        xb[m, 1] = imag.astype(BF16)
        term = jnp.concatenate([wr * real - wi * imag, -wr * imag - wi * real], axis=0).T
        high = term.astype(BF16)
        yt[0:128, 128 * m : 128 * m + 128] = high
        yt[128:256, 128 * m : 128 * m + 128] = (term - high.astype(F32)).astype(BF16)

    for i in range(HELD):
        send_home(i)
    wait_in(prow.at[0], cg_recv)
    wait_in(prow.at[0:3], cr_recv)
    for n in range(4):
        columns = jnp.concatenate([prow[2 * n].reshape(1024, 128), prow[2 * n + 1].reshape(1024, 128)], axis=1)
        two = jnp.dot(yt[...], columns, preferred_element_type=F32)
        one = two[:128] + two[128:]
        d[4 * n : 4 * n + 2] = one[:, :128].T.reshape(2, 64, 128)
        d[4 * n + 2 : 4 * n + 4] = one[:, 128:].T.reshape(2, 64, 128)

    for h in range(2):
        for k in (2, 1, 3):
            pole, grid = at_x(k)
            there = pl.ds(pl.multiple_of(lax.rem(x + k, 4) * 16 + 8 * h, 8), 8)
            remote(d.at[:, there], rx.at[h, k - 1], xr_send, xr_recv.at[h], pole, grid).start()

    for h in range(2):
        wait_in(rx.at[h], xr_recv.at[h])
        here = pl.ds(pl.multiple_of(x * 16 + 8 * h, 8), 8)
        fb[h] = d[:, here] + rx[h, 0] + rx[h, 1] + rx[h, 2]

        def send_z(n):
            to = lax.rem(z + jnp.where(n % 2 == 0, 8 + n // 2, 7 - n // 2), 16)
            remote(fb.at[h, to], rz.at[h, z], z_send.at[h], z_recv.at[h], p, 2 * to + xl).start()

        each(15, send_z)
    for i in range(HELD, 8):
        send_home(i)

    @pl.when(xl == xh)
    def _():
        wait_in(dg.at[0:15], g_recv)
        wait_out(dg.at[0:15], g_send)

    @pl.when(xl != xh)
    def _():
        wait_in(dg, g_recv)
        wait_out(dg, g_send)

    wait_out(left, l_send)
    wait_out(panel, p_send)

    @pl.when(xh == 0)
    def _():
        for n in range(2):
            wait_out(ar, h_send.at[n])

    @pl.when(z == p)
    def _():
        def done_w(q):
            @pl.when(q != p)
            def _():
                wait_out(wt, w_send.at[q])

        each(16, done_w)

    def done_a(n):
        @pl.when(2 * n + pole_core != z)
        def _():
            wait_out(ar, a_send.at[n])

    each(8, done_a)

    wait_out(pr.at[0:4], pz_send.at[1])
    wait_out(lbuf.at[:, 0:64, 0:256], ly_send.at[0])
    wait_out(lbuf.at[:, 0:64, 0:128], ly_send.at[1])
    wait_out(rows_here, lc_send)
    wait_out(prow.at[0:3], xg_send)
    wait_out(prow.at[0:3], yg_send)
    wait_out(prow.at[0], cg_send)
    wait_out(prow.at[0:3], cr_send)
    wait_out(rx, xr_send)

    total = dg[0]
    for n in range(1, 16):
        total = total + dg[n]
    for h in range(2):
        rz[h, z] = fb[h, z]
        wait_in(rz.at[h, 0:15], z_recv.at[h])
        minus = rz[h, 0]
        for n in range(1, 16):
            minus = minus + rz[h, n]
        res[8 * h : 8 * h + 8] = total[8 * h : 8 * h + 8] - minus

    place = dens.at[aligned(xl, 16), aligned(u, 128)]

    def send_n(k):
        n = lax.rem(p + k, 16)

        @pl.when(other(n, 2 * z + xh))
        def _():
            remote(res, place, n_send, n_recv, n, 2 * z + xh).start()

    each(16, send_n)

    @pl.when(xl == xh)
    def _():
        copy = pltpu.make_async_copy(res, place, one_sem.at[2])
        copy.start()
        copy.wait()

    wait_out(xb, r_send)
    for h in range(2):
        wait_out(fb.at[h, 0:15], z_send.at[h])

    @pl.when(xl == xh)
    def _():
        wait_out(dg.at[0:15], n_send)
        wait_in(dg.at[0:15], n_recv)

    @pl.when(xl != xh)
    def _():
        wait_out(dg, n_send)
        wait_in(dg, n_recv)

    wait_in(xb, o_recv)


def shards(panel, inverse_blocks, diag_inverse, ancestors, pole_index, weight_table):
    vmem = pl.BlockSpec(memory_space=pltpu.VMEM)
    smem = pl.BlockSpec(memory_space=pltpu.SMEM)
    hbm = pl.BlockSpec(memory_space=pl.ANY)
    dma = pltpu.SemaphoreType.DMA
    scratch = [
        pltpu.VMEM((1, 2, 64, 1024), BF16),
        pltpu.VMEM((1, 1, 8, 2, 64, 64), BF16),
        pltpu.VMEM((1, 32, 2048), F32),
        pltpu.VMEM((128, 512), BF16),
        pltpu.VMEM((8, 128), F32),
        pltpu.VMEM((1, 8), jnp.int32),
        pltpu.VMEM((8, 2, 64, 128), BF16),
        pltpu.VMEM((8, 64, 128), BF16),
        pltpu.VMEM((8, 4, 2, 64, 128), BF16),
        pltpu.VMEM((8, 128, 512), BF16),
        pltpu.VMEM((8, 1, 8), jnp.int32),
        pltpu.SMEM((8, 1, 8), jnp.int32),
        pltpu.VMEM((8, 128), F32),
        pltpu.VMEM((8, 8, 2, 64, 128), BF16),
        pltpu.VMEM((8, 2, 64, 128), BF16),
        pltpu.VMEM((256, 1024), BF16),
        pltpu.VMEM((16, 64, 128), F32),
        pltpu.VMEM((2, 3, 16, 8, 128), F32),
        pltpu.VMEM((2, 16, 8, 128), F32),
        pltpu.VMEM((2, 16, 8, 128), F32),
        pltpu.VMEM((8, 32, 128), F32),
        pltpu.VMEM((16, 16, 128), F32),
        pltpu.VMEM((16, 128), F32),
        pltpu.SemaphoreType.REGULAR((3,)), dma((3,)), dma((3,)),
        dma, dma((8,)), dma, dma((8,)), dma((2,)), dma, dma((2,)), dma((8,)), dma, dma((8,)), dma((8,)), dma((8,)), dma((16,)), dma,
        dma, dma((3, 8)), dma, dma((3, 8)), dma, dma, dma, dma,
        dma((2,)), dma((4,)), dma, dma,
        dma, dma, dma, dma, dma, dma((2,)), dma((2,)), dma((2,)), dma, dma,
    ]
    return pl.pallas_call(
        kernel,
        out_shape=(
            jax.ShapeDtypeStruct(panel.shape, BF16),
            jax.ShapeDtypeStruct((32, 1024), F32),
        ),
        in_specs=[vmem, smem, smem, hbm, hbm, hbm],
        out_specs=(hbm, hbm),
        scratch_shapes=scratch,
        compiler_params=pltpu.CompilerParams(
            collective_id=1, has_side_effects=True, vmem_limit_bytes=VMEM
        ),
    )(ancestors, pole_index, weight_table.T, panel, inverse_blocks, diag_inverse)


def solution(mesh):
    placed = (
        P("pole", None, "grid", None),
        P("pole", "grid", None, None, None, None),
        P("pole", "grid", None),
        P("grid", None),
        P("pole"),
        P(),
    )
    return jax.shard_map(
        shards,
        mesh=mesh,
        in_specs=placed,
        out_specs=(P("pole", None, "grid", None), P("grid", None)),
        check_vma=False,
    )
```

```python
import jax
import jax.numpy as jnp
from jax import lax
from jax.experimental import pallas as pl
from jax.experimental.pallas import tpu as pltpu
from jax.sharding import PartitionSpec as P

MESH = pl.DeviceIdType.MESH
F32 = jnp.float32
BF16 = jnp.bfloat16
VMEM = 60 << 20
HOME = ((8, 6, 10, 4, 12, 2, 14, 0), (7, 9, 5, 11, 3, 13, 1, 15))
HELD = 5
DIRECT = 5
FAR = ((0, 4, 12, 8, 6, 10, 2, 14), (1, 15, 7, 9, 5, 11, 3, 13))


def kernel(
    anc_v, pole_s, table_s, panel_h, inv_h, diag_h,
    off, dens,
    panel, inv, diag, left, wt, ar, pr, lr, buf, lbuf, ancb_v, ancb_s, wtb, prow, xb, yt, d, rx, fb, rz, wd, dg, res,
    reach_sem, in_sem, one_sem,
    p_send, p_recv, l_send, l_recv, h_send, h_recv, pz_send, pz_recv, lz_send, lz_recv, a_send, a_recv, w_send, w_recv,
    xg_send, xg_recv, yg_send, yg_recv, cg_send, cg_recv, cr_send, cr_recv,
    ly_send, ly_recv, lc_send, lc_recv,
    g_send, g_recv, r_send, o_recv, xr_send, xr_recv, z_send, z_recv, n_send, n_recv,
):
    g = lax.axis_index("grid")
    p = lax.axis_index("pole")
    z, xl = g // 2, g % 2
    y, xh, core = p // 4, (p // 2) % 2, p % 2
    u = 2 * y + core
    x = 2 * xh + xl
    half = z // 2
    odd = z % 2
    own_parity = 1 - lax.rem(xh + xl, 2)
    part = lax.rem(x + 3 + 2 * odd, 4)
    parity = part // 2
    pole_core = lax.rem(z + own_parity, 2)
    passed_part = 2 * odd + 1 - xl
    partner = p + 1 - 2 * core
    gx = g + 1 - 2 * xl

    def remote(src, dst, send, recv, pole, grid):
        return pltpu.make_async_remote_copy(
            src_ref=src, dst_ref=dst, send_sem=send, recv_sem=recv,
            device_id={"pole": pole, "grid": grid}, device_id_type=MESH,
        )

    def wait_in(ref, sem):
        remote(ref, ref, sem, sem, partner, g).wait_recv()

    def wait_out(ref, sem):
        remote(ref, ref, sem, sem, partner, g).wait_send()

    def other(pole, grid):
        return jnp.logical_or(pole != p, grid != g)

    def each(count, body):
        def step(n, carry):
            body(n)
            return carry

        lax.fori_loop(0, count, step, 0)

    def aligned(n, size):
        return pl.ds(pl.multiple_of(n * size, size), size)

    barrier = pltpu.get_barrier_semaphore()

    def hello(pole, grid):
        @pl.when(other(pole, grid))
        def _():
            pl.semaphore_signal(barrier, inc=1, device_id={"pole": pole, "grid": grid}, device_id_type=MESH)

    loads = [
        pltpu.make_async_copy(inv_h, inv, in_sem.at[0]),
        pltpu.make_async_copy(panel_h, panel, in_sem.at[1]),
        pltpu.make_async_copy(diag_h, diag, in_sem.at[2]),
    ]
    for load in loads:
        load.start()
    next_z, last_z = [2 * lax.rem(z + k, 16) + xl for k in (1, 15)]
    hello(p, next_z)
    hello(p, last_z)
    each(32, lambda n: hello(n // 2, 2 * z + n % 2))
    loads[0].wait()
    for k in range(0, 8, 2):
        left[:, 64 * k : 64 * k + 128] = jnp.concatenate(
            [inv[0, 0, k].reshape(128, 64), inv[0, 0, k + 1].reshape(128, 64)], axis=1
        )
    loads[1].wait()
    pl.semaphore_wait(barrier, 2 + 31)

    def reach(n):
        for k in (1 << n, 16 - (1 << n)):
            pl.semaphore_signal(
                reach_sem.at[n], inc=1,
                device_id={"pole": p, "grid": 2 * lax.rem(z + k, 16) + xl}, device_id_type=MESH,
            )

    reach(0)

    def target(n):
        return (n // 2) * 4 + lax.rem(xl + odd + core, 2) * 2 + n % 2

    def send_l(k):
        n = lax.rem(u + k, 8)
        piece = left.at[aligned(n % 2, 64), aligned(n // 2, 128)]
        remote(piece, lr.at[p // 2], l_send, l_recv.at[p // 2], target(n), gx).start()

    def send_p(k):
        n = lax.rem(u + k, 8)
        remote(panel.at[0, :, :, aligned(n, 128)], pr.at[p // 2], p_send, p_recv.at[p // 2], target(n), gx).start()

    @pl.when(xh == 0)
    def _():
        for n in range(2):
            remote(anc_v, ar, h_send.at[n], h_recv, target(2 * y + n), gx).start()

    each(8, send_l)
    each(8, send_p)
    for n in range(3):
        pl.semaphore_wait(reach_sem.at[n], 2)
        if n < 2:
            reach(n + 1)

    index = pole_s[0]
    my_wr = table_s[0, index]
    my_wi = table_s[1, index]
    is_real = lax.broadcasted_iota(jnp.int32, (8, 128), 0) == 0
    wt[...] = jnp.where(is_real, my_wr, my_wi)

    @pl.when(z == p)
    def _():
        def send_w(q):
            @pl.when(q != p)
            def _():
                remote(wt, wtb, w_send.at[q], w_recv, q, g).start()

        wtb[...] = wt[...]
        each(16, send_w)

    l_place = (aligned(core, 64), aligned(y, 128))

    def pole_of(n):
        from_u = lax.rem(u + 8 - 2 * (n // 2) - lax.rem(core + pole_core, 2), 8)
        return (from_u // 2) * 4 + (n % 2) * 2 + pole_core

    def pole_far(n):
        return lax.rem(z + jnp.where(own_parity == 0, FAR[0][n], FAR[1][n]), 16)

    def pass_l(n):
        q = pole_of(n)
        ref = lr.at[q // 2]
        wait_in(ref, l_recv.at[q // 2])

        @pl.when(q != z)
        def _():
            remote(ref, lbuf.at[(half,) + l_place], lz_send, lz_recv.at[half], p, 2 * q + xl).start()

    def pass_p(n):
        q = pole_far(n)
        ref = pr.at[q // 2]
        wait_in(ref, p_recv.at[q // 2])

        @pl.when(q != z)
        def _():
            remote(ref, buf.at[half, passed_part], pz_send.at[(0, 0, 1, 1, 2, 2, 2, 2)[n]], pz_recv.at[half], p, 2 * q + xl).start()

    def pass_a(n):
        q = 2 * n + pole_core

        @pl.when(q != z)
        def _():
            remote(ar, ancb_v.at[half], a_send.at[n], a_recv.at[half], p, 2 * q + xl).start()

    def sent(ref, sem, count):
        @pl.when(own_parity == 0)
        def _():
            wait_out(ref.at[0 : count - 1], sem)

        @pl.when(own_parity != 0)
        def _():
            wait_out(ref.at[0:count], sem)

    each(8, pass_l)
    sent(lr, lz_send, 8)
    for n in range(4):
        pass_p(n)
    wait_in(ar, h_recv)
    each(8, pass_a)

    @pl.when(own_parity == 0)
    def _():
        copies = [
            pltpu.make_async_copy(lr.at[half], lbuf.at[(half,) + l_place], one_sem.at[1]),
            pltpu.make_async_copy(ar, ancb_v.at[half], one_sem.at[2]),
        ]
        for copy in copies:
            copy.start()
        for copy in copies:
            copy.wait()

    loads[2].wait()
    for n in range(8):
        wd[n] = my_wr * diag[0, :, 128 * n : 128 * n + 128] - my_wi * diag[0, :, 1024 + 128 * n : 1152 + 128 * n]

    def holder(n):
        return (n // 4) * 4 + xl * 2 + (n // 2) % 2, 2 * z + n % 2

    def send_d(n):
        pole, grid = holder(n)

        @pl.when(other(pole, grid))
        def _():
            remote(wd.at[n // 2, aligned(n % 2, 16)], dg.at[p], g_send, g_recv, pole, grid).start()

    each(16, send_d)

    @pl.when(xl == xh)
    def _():
        dg[p] = wd[u, aligned(xl, 16)]

    def at_x(k):
        to = lax.rem(x + k, 4)
        return y * 4 + (to // 2) * 2 + core, 2 * z + to % 2

    def at_y(k):
        return lax.rem(y + k, 4) * 4 + xh * 2 + core

    def from_z(m, ref, sem):
        @pl.when(2 * m + parity != z)
        def _():
            wait_in(ref, sem.at[m])

    for m in range(8):
        from_z(m, lbuf.at[(m,) + l_place], lz_recv)

    def l_of(k, rows):
        return lbuf.at[rows, aligned(core, 64), aligned(lax.rem(y + k, 4), 128)]

    whole = slice(0, 8)
    for k, n in ((1, 0), (3, 1)):
        ref = l_of(0, whole)
        remote(ref, ref, ly_send.at[0], ly_recv.at[n], at_y(k), g).start()
    sent(pr, pz_send.at[0], 2)
    for n in range(4, 8):
        pass_p(n)

    @pl.when(own_parity == 0)
    def _():
        copy = pltpu.make_async_copy(pr.at[half], buf.at[half, part], one_sem.at[0])
        copy.start()
        copy.wait()

    for k, n, to, rows in ((3, 0, 1, slice(0, 4)), (1, 1, 3, slice(4, 8))):
        wait_in(l_of(k, whole), ly_recv.at[n])
        ref = l_of(k, rows)
        remote(ref, ref, ly_send.at[1], ly_recv.at[2 + n], at_y(to), g).start()
    for m in range(8):
        from_z(m, ancb_v.at[m], a_recv)
    small = pltpu.make_async_copy(ancb_v, ancb_s, one_sem.at[0])
    small.start()

    def far_m(own, i):
        return lax.rem(z + 16 - jnp.where(own == 0, FAR[0][i], FAR[1][i]), 16) // 2

    def x_part(k):
        return lax.rem(part + k, 4)

    def x_own(k):
        to = lax.rem(x + k, 4)
        return 1 - lax.rem(to // 2 + to % 2, 2)

    def y_part(k):
        return 2 * lax.rem(y + k, 4) + core

    ways = ((1, 0), (3, 1))
    rows_here = lbuf.at[:, aligned(core, 64), :]

    def start_one(i):
        m = far_m(own_parity, i)
        block = buf.at[m, part]
        there = prow.at[u, m]
        for k, n in ways + (((2, 2),) if i >= DIRECT else ()):
            pole, grid = at_x(k)
            remote(block, block, xg_send, xg_recv.at[n, i], pole, grid).start()
            remote(block, there, yg_send, yg_recv.at[n, i], at_y(k), g).start()
        remote(block, there, cg_send, cg_recv, partner, g).start()
        prow[u, m] = buf[m, part]

    def pass_one(i):
        m = far_m(own_parity, i)
        for k, n in ((3, 0), (1, 1)):
            ref = buf.at[far_m(x_own(k), i), x_part(k)]
            wait_in(ref, xg_recv.at[n, i])
            if i < DIRECT and i % 2 == n:
                pole, grid = at_x(4 - k)
                remote(ref, ref, xg_send, xg_recv.at[2, i], pole, grid).start()
        for k, n in ((3, 0), (1, 1)):
            ref = prow.at[y_part(k), m]
            wait_in(ref, yg_recv.at[n, i])
            if i < DIRECT and i % 2 == n:
                remote(ref, ref, yg_send, yg_recv.at[2, i], at_y(4 - k), g).start()

    def arrived(i):
        from_z(far_m(own_parity, i), buf.at[far_m(own_parity, i), part], pz_recv)

    for i in range(4):
        arrived(i)
        start_one(i)
    for n, rows in ((0, slice(0, 4)), (1, slice(4, 8))):
        wait_in(l_of(2, rows), ly_recv.at[2 + n])
    remote(rows_here, rows_here, lc_send, lc_recv, partner, g).start()
    for i in range(4, 8):
        pass_one(i - 4)
        arrived(i)
        start_one(i)
    for i in range(4, 8):
        pass_one(i)

    def send_cr(k):
        came = prow.at[y_part(k)]
        remote(came, came, cr_send, cr_recv, partner, g).start()

    send_cr(3)
    send_cr(1)
    for i in range(8):
        wait_in(buf.at[far_m(x_own(2), i), x_part(2)], xg_recv.at[2, i])
    for i in range(8):
        wait_in(prow.at[y_part(2), far_m(own_parity, i)], yg_recv.at[2, i])
    send_cr(2)
    small.wait()
    wait_in(rows_here, lc_recv)

    @pl.when(z != p)
    def _():
        wait_in(wtb, w_recv)

    wr = wtb[0:1, :]
    wi = wtb[1:2, :]
    off_place = off.at[0, :, :, aligned(u, 128)]

    def send_home(i):
        m = lax.rem(z + 16 - jnp.where(own_parity == 0, HOME[0][i], HOME[1][i]), 16) // 2
        remote(xb.at[m], off_place, r_send, o_recv, z, 2 * (2 * m + parity) + 1 - xl).start()

    for m in range(8):
        rows = []
        for k in range(8):
            j = ancb_s[m, 0, k]
            rows.append(jnp.concatenate([buf[j // 4, j % 4, 0], buf[j // 4, j % 4, 1]], axis=1))
        both = jnp.dot(lbuf[m], jnp.concatenate(rows, axis=0), preferred_element_type=F32)
        real = both[64:, 128:] - both[:64, :128]
        imag = -(both[:64, 128:] + both[64:, :128])
        xb[m, 0] = real.astype(BF16)
        xb[m, 1] = imag.astype(BF16)
        term = jnp.concatenate([wr * real - wi * imag, -wr * imag - wi * real], axis=0).T
        high = term.astype(BF16)
        yt[0:128, 128 * m : 128 * m + 128] = high
        yt[128:256, 128 * m : 128 * m + 128] = (term - high.astype(F32)).astype(BF16)

    for i in range(HELD):
        send_home(i)
    wait_in(prow.at[0], cg_recv)
    wait_in(prow.at[0:3], cr_recv)
    for n in range(4):
        columns = jnp.concatenate([prow[2 * n].reshape(1024, 128), prow[2 * n + 1].reshape(1024, 128)], axis=1)
        two = jnp.dot(yt[...], columns, preferred_element_type=F32)
        one = two[:128] + two[128:]
        d[4 * n : 4 * n + 2] = one[:, :128].T.reshape(2, 64, 128)
        d[4 * n + 2 : 4 * n + 4] = one[:, 128:].T.reshape(2, 64, 128)

    for h in range(2):
        for k in (2, 1, 3):
            pole, grid = at_x(k)
            there = pl.ds(pl.multiple_of(lax.rem(x + k, 4) * 16 + 8 * h, 8), 8)
            remote(d.at[:, there], rx.at[h, k - 1], xr_send, xr_recv.at[h], pole, grid).start()

    for h in range(2):
        wait_in(rx.at[h], xr_recv.at[h])
        here = pl.ds(pl.multiple_of(x * 16 + 8 * h, 8), 8)
        fb[h] = d[:, here] + rx[h, 0] + rx[h, 1] + rx[h, 2]

        def send_z(n):
            to = lax.rem(z + jnp.where(n % 2 == 0, 8 + n // 2, 7 - n // 2), 16)
            remote(fb.at[h, to], rz.at[h, z], z_send.at[h], z_recv.at[h], p, 2 * to + xl).start()

        each(15, send_z)
    for i in range(HELD, 8):
        send_home(i)

    @pl.when(xl == xh)
    def _():
        wait_in(dg.at[0:15], g_recv)
        wait_out(dg.at[0:15], g_send)

    @pl.when(xl != xh)
    def _():
        wait_in(dg, g_recv)
        wait_out(dg, g_send)

    wait_out(left, l_send)
    wait_out(panel, p_send)

    @pl.when(xh == 0)
    def _():
        for n in range(2):
            wait_out(ar, h_send.at[n])

    @pl.when(z == p)
    def _():
        def done_w(q):
            @pl.when(q != p)
            def _():
                wait_out(wt, w_send.at[q])

        each(16, done_w)

    def done_a(n):
        @pl.when(2 * n + pole_core != z)
        def _():
            wait_out(ar, a_send.at[n])

    each(8, done_a)

    wait_out(pr.at[0:2], pz_send.at[1])
    wait_out(pr.at[0:4], pz_send.at[2])
    wait_out(lbuf.at[:, 0:64, 0:256], ly_send.at[0])
    wait_out(lbuf.at[:, 0:64, 0:128], ly_send.at[1])
    wait_out(rows_here, lc_send)
    wait_out(prow.at[0:3], xg_send)
    wait_out(prow.at[0:3], yg_send)
    wait_out(prow.at[0], cg_send)
    wait_out(prow.at[0:3], cr_send)
    wait_out(rx, xr_send)

    total = dg[0]
    for n in range(1, 16):
        total = total + dg[n]
    for h in range(2):
        rz[h, z] = fb[h, z]
        wait_in(rz.at[h, 0:15], z_recv.at[h])
        minus = rz[h, 0]
        for n in range(1, 16):
            minus = minus + rz[h, n]
        res[8 * h : 8 * h + 8] = total[8 * h : 8 * h + 8] - minus

    place = dens.at[aligned(xl, 16), aligned(u, 128)]

    def send_n(k):
        n = lax.rem(p + k, 16)

        @pl.when(other(n, 2 * z + xh))
        def _():
            remote(res, place, n_send, n_recv, n, 2 * z + xh).start()

    each(16, send_n)

    @pl.when(xl == xh)
    def _():
        copy = pltpu.make_async_copy(res, place, one_sem.at[2])
        copy.start()
        copy.wait()

    wait_out(xb, r_send)
    for h in range(2):
        wait_out(fb.at[h, 0:15], z_send.at[h])

    @pl.when(xl == xh)
    def _():
        wait_out(dg.at[0:15], n_send)
        wait_in(dg.at[0:15], n_recv)

    @pl.when(xl != xh)
    def _():
        wait_out(dg, n_send)
        wait_in(dg, n_recv)

    wait_in(xb, o_recv)


def shards(panel, inverse_blocks, diag_inverse, ancestors, pole_index, weight_table):
    vmem = pl.BlockSpec(memory_space=pltpu.VMEM)
    smem = pl.BlockSpec(memory_space=pltpu.SMEM)
    hbm = pl.BlockSpec(memory_space=pl.ANY)
    dma = pltpu.SemaphoreType.DMA
    scratch = [
        pltpu.VMEM((1, 2, 64, 1024), BF16),
        pltpu.VMEM((1, 1, 8, 2, 64, 64), BF16),
        pltpu.VMEM((1, 32, 2048), F32),
        pltpu.VMEM((128, 512), BF16),
        pltpu.VMEM((8, 128), F32),
        pltpu.VMEM((1, 8), jnp.int32),
        pltpu.VMEM((8, 2, 64, 128), BF16),
        pltpu.VMEM((8, 64, 128), BF16),
        pltpu.VMEM((8, 4, 2, 64, 128), BF16),
        pltpu.VMEM((8, 128, 512), BF16),
        pltpu.VMEM((8, 1, 8), jnp.int32),
        pltpu.SMEM((8, 1, 8), jnp.int32),
        pltpu.VMEM((8, 128), F32),
        pltpu.VMEM((8, 8, 2, 64, 128), BF16),
        pltpu.VMEM((8, 2, 64, 128), BF16),
        pltpu.VMEM((256, 1024), BF16),
        pltpu.VMEM((16, 64, 128), F32),
        pltpu.VMEM((2, 3, 16, 8, 128), F32),
        pltpu.VMEM((2, 16, 8, 128), F32),
        pltpu.VMEM((2, 16, 8, 128), F32),
        pltpu.VMEM((8, 32, 128), F32),
        pltpu.VMEM((16, 16, 128), F32),
        pltpu.VMEM((16, 128), F32),
        pltpu.SemaphoreType.REGULAR((3,)), dma((3,)), dma((3,)),
        dma, dma((8,)), dma, dma((8,)), dma((2,)), dma, dma((3,)), dma((8,)), dma, dma((8,)), dma((8,)), dma((8,)), dma((16,)), dma,
        dma, dma((3, 8)), dma, dma((3, 8)), dma, dma, dma, dma,
        dma((2,)), dma((4,)), dma, dma,
        dma, dma, dma, dma, dma, dma((2,)), dma((2,)), dma((2,)), dma, dma,
    ]
    return pl.pallas_call(
        kernel,
        out_shape=(
            jax.ShapeDtypeStruct(panel.shape, BF16),
            jax.ShapeDtypeStruct((32, 1024), F32),
        ),
        in_specs=[vmem, smem, smem, hbm, hbm, hbm],
        out_specs=(hbm, hbm),
        scratch_shapes=scratch,
        compiler_params=pltpu.CompilerParams(
            collective_id=1, has_side_effects=True, vmem_limit_bytes=VMEM
        ),
    )(ancestors, pole_index, weight_table.T, panel, inverse_blocks, diag_inverse)


def solution(mesh):
    placed = (
        P("pole", None, "grid", None),
        P("pole", "grid", None, None, None, None),
        P("pole", "grid", None),
        P("grid", None),
        P("pole"),
        P(),
    )
    return jax.shard_map(
        shards,
        mesh=mesh,
        in_specs=placed,
        out_specs=(P("pole", None, "grid", None), P("grid", None)),
        check_vma=False,
    )
```

```python
import jax
import jax.numpy as jnp
from jax import lax
from jax.experimental import pallas as pl
from jax.experimental.pallas import tpu as pltpu
from jax.sharding import PartitionSpec as P

MESH = pl.DeviceIdType.MESH
F32 = jnp.float32
BF16 = jnp.bfloat16
VMEM = 60 << 20
HOME = ((8, 6, 10, 4, 12, 2, 14, 0), (7, 9, 5, 11, 3, 13, 1, 15))
HELD = 5
DIRECT = 5
FAR = ((0, 4, 12, 8, 6, 10, 2, 14), (1, 15, 7, 9, 5, 11, 3, 13))


def kernel(
    anc_v, pole_s, table_s, panel_h, inv_h, diag_h,
    off, dens,
    panel, inv, diag, left, wt, ar, pr, lr, buf, lbuf, ancb_v, ancb_s, wtb, prow, xb, yt, d, rx, fb, rz, wd, dg, res,
    reach_sem, in_sem, one_sem,
    p_send, p_recv, l_send, l_recv, h_send, h_recv, pz_send, pz_recv, lz_send, lz_recv, a_send, a_recv, w_send, w_recv,
    xg_send, xg_recv, yg_send, yg_recv, cg_send, cg_recv, cr_send, cr_recv,
    ly_send, ly_recv, lc_send, lc_recv,
    g_send, g_recv, r_send, o_recv, xr_send, xr_recv, z_send, z_recv, n_send, n_recv,
):
    g = lax.axis_index("grid")
    p = lax.axis_index("pole")
    z, xl = g // 2, g % 2
    y, xh, core = p // 4, (p // 2) % 2, p % 2
    u = 2 * y + core
    x = 2 * xh + xl
    half = z // 2
    odd = z % 2
    own_parity = 1 - lax.rem(xh + xl, 2)
    part = lax.rem(x + 3 + 2 * odd, 4)
    parity = part // 2
    pole_core = lax.rem(z + own_parity, 2)
    passed_part = 2 * odd + 1 - xl
    partner = p + 1 - 2 * core
    gx = g + 1 - 2 * xl

    def remote(src, dst, send, recv, pole, grid):
        return pltpu.make_async_remote_copy(
            src_ref=src, dst_ref=dst, send_sem=send, recv_sem=recv,
            device_id={"pole": pole, "grid": grid}, device_id_type=MESH,
        )

    def wait_in(ref, sem):
        remote(ref, ref, sem, sem, partner, g).wait_recv()

    def wait_out(ref, sem):
        remote(ref, ref, sem, sem, partner, g).wait_send()

    def other(pole, grid):
        return jnp.logical_or(pole != p, grid != g)

    def each(count, body):
        def step(n, carry):
            body(n)
            return carry

        lax.fori_loop(0, count, step, 0)

    def aligned(n, size):
        return pl.ds(pl.multiple_of(n * size, size), size)

    barrier = pltpu.get_barrier_semaphore()

    def hello(pole, grid):
        @pl.when(other(pole, grid))
        def _():
            pl.semaphore_signal(barrier, inc=1, device_id={"pole": pole, "grid": grid}, device_id_type=MESH)

    loads = [
        pltpu.make_async_copy(inv_h, inv, in_sem.at[0]),
        pltpu.make_async_copy(panel_h, panel, in_sem.at[1]),
        pltpu.make_async_copy(diag_h, diag, in_sem.at[2]),
    ]
    for load in loads:
        load.start()
    next_z, last_z = [2 * lax.rem(z + k, 16) + xl for k in (1, 15)]
    hello(p, next_z)
    hello(p, last_z)
    each(32, lambda n: hello(n // 2, 2 * z + n % 2))
    loads[0].wait()
    for k in range(0, 8, 2):
        left[:, 64 * k : 64 * k + 128] = jnp.concatenate(
            [inv[0, 0, k].reshape(128, 64), inv[0, 0, k + 1].reshape(128, 64)], axis=1
        )
    loads[1].wait()
    pl.semaphore_wait(barrier, 2 + 31)

    def reach(n):
        for k in (1 << n, 16 - (1 << n)):
            pl.semaphore_signal(
                reach_sem.at[n], inc=1,
                device_id={"pole": p, "grid": 2 * lax.rem(z + k, 16) + xl}, device_id_type=MESH,
            )

    reach(0)

    def target(n):
        return (n // 2) * 4 + lax.rem(xl + odd + core, 2) * 2 + n % 2

    def send_l(k):
        n = lax.rem(u + k, 8)
        piece = left.at[aligned(n % 2, 64), aligned(n // 2, 128)]
        remote(piece, lr.at[p // 2], l_send, l_recv.at[p // 2], target(n), gx).start()

    def send_p(k):
        n = lax.rem(u + k, 8)
        remote(panel.at[0, :, :, aligned(n, 128)], pr.at[p // 2], p_send, p_recv.at[p // 2], target(n), gx).start()

    @pl.when(xh == 0)
    def _():
        for n in range(2):
            remote(anc_v, ar, h_send.at[n], h_recv, target(2 * y + n), gx).start()

    each(8, send_l)
    each(8, send_p)
    for n in range(3):
        pl.semaphore_wait(reach_sem.at[n], 2)
        if n < 2:
            reach(n + 1)

    index = pole_s[0]
    my_wr = table_s[0, index]
    my_wi = table_s[1, index]
    is_real = lax.broadcasted_iota(jnp.int32, (8, 128), 0) == 0
    wt[...] = jnp.where(is_real, my_wr, my_wi)

    @pl.when(z == p)
    def _():
        def send_w(q):
            @pl.when(q != p)
            def _():
                remote(wt, wtb, w_send.at[q], w_recv, q, g).start()

        wtb[...] = wt[...]
        each(16, send_w)

    l_place = (aligned(core, 64), aligned(y, 128))

    def pole_of(n):
        from_u = lax.rem(u + 8 - 2 * (n // 2) - lax.rem(core + pole_core, 2), 8)
        return (from_u // 2) * 4 + (n % 2) * 2 + pole_core

    def pole_far(n):
        return lax.rem(z + jnp.where(own_parity == 0, FAR[0][n], FAR[1][n]), 16)

    def pass_l(n):
        q = pole_of(n)
        ref = lr.at[q // 2]
        wait_in(ref, l_recv.at[q // 2])

        @pl.when(q != z)
        def _():
            remote(ref, lbuf.at[(half,) + l_place], lz_send, lz_recv.at[half], p, 2 * q + xl).start()

    def pass_p(n):
        q = pole_far(n)
        ref = pr.at[q // 2]
        wait_in(ref, p_recv.at[q // 2])

        @pl.when(q != z)
        def _():
            remote(ref, buf.at[half, passed_part], pz_send.at[(0, 0, 1, 1, 2, 2, 2, 2)[n]], pz_recv.at[half], p, 2 * q + xl).start()

    def pass_a(n):
        q = 2 * n + pole_core

        @pl.when(q != z)
        def _():
            remote(ar, ancb_v.at[half], a_send.at[n], a_recv.at[half], p, 2 * q + xl).start()

    def sent(ref, sem, count):
        @pl.when(own_parity == 0)
        def _():
            wait_out(ref.at[0 : count - 1], sem)

        @pl.when(own_parity != 0)
        def _():
            wait_out(ref.at[0:count], sem)

    each(8, pass_l)
    sent(lr, lz_send, 8)
    for n in range(4):
        pass_p(n)
    wait_in(ar, h_recv)
    each(8, pass_a)

    @pl.when(own_parity == 0)
    def _():
        copies = [
            pltpu.make_async_copy(lr.at[half], lbuf.at[(half,) + l_place], one_sem.at[1]),
            pltpu.make_async_copy(ar, ancb_v.at[half], one_sem.at[2]),
        ]
        for copy in copies:
            copy.start()
        for copy in copies:
            copy.wait()

    loads[2].wait()
    for n in range(8):
        wd[n] = my_wr * diag[0, :, 128 * n : 128 * n + 128] - my_wi * diag[0, :, 1024 + 128 * n : 1152 + 128 * n]

    def holder(n):
        return (n // 4) * 4 + xl * 2 + (n // 2) % 2, 2 * z + n % 2

    def send_d(n):
        pole, grid = holder(n)

        @pl.when(other(pole, grid))
        def _():
            remote(wd.at[n // 2, aligned(n % 2, 16)], dg.at[p], g_send, g_recv, pole, grid).start()

    each(16, send_d)

    @pl.when(xl == xh)
    def _():
        dg[p] = wd[u, aligned(xl, 16)]

    def at_x(k):
        to = lax.rem(x + k, 4)
        return y * 4 + (to // 2) * 2 + core, 2 * z + to % 2

    def at_y(k):
        return lax.rem(y + k, 4) * 4 + xh * 2 + core

    def from_z(m, ref, sem):
        @pl.when(2 * m + parity != z)
        def _():
            wait_in(ref, sem.at[m])

    for m in range(8):
        from_z(m, lbuf.at[(m,) + l_place], lz_recv)

    def l_of(k, rows):
        return lbuf.at[rows, aligned(core, 64), aligned(lax.rem(y + k, 4), 128)]

    whole = slice(0, 8)
    for k, n in ((1, 0), (3, 1)):
        ref = l_of(0, whole)
        remote(ref, ref, ly_send.at[0], ly_recv.at[n], at_y(k), g).start()
    sent(pr, pz_send.at[0], 2)
    for n in range(4, 8):
        pass_p(n)

    @pl.when(own_parity == 0)
    def _():
        copy = pltpu.make_async_copy(pr.at[half], buf.at[half, part], one_sem.at[0])
        copy.start()
        copy.wait()

    for k, n, to, rows in ((3, 0, 1, slice(0, 4)), (1, 1, 3, slice(4, 8))):
        wait_in(l_of(k, whole), ly_recv.at[n])
        ref = l_of(k, rows)
        remote(ref, ref, ly_send.at[1], ly_recv.at[2 + n], at_y(to), g).start()
    for m in range(8):
        from_z(m, ancb_v.at[m], a_recv)
    small = pltpu.make_async_copy(ancb_v, ancb_s, one_sem.at[0])
    small.start()

    def far_m(own, i):
        return lax.rem(z + 16 - jnp.where(own == 0, FAR[0][i], FAR[1][i]), 16) // 2

    def x_part(k):
        return lax.rem(part + k, 4)

    def x_own(k):
        to = lax.rem(x + k, 4)
        return 1 - lax.rem(to // 2 + to % 2, 2)

    def y_part(k):
        return 2 * lax.rem(y + k, 4) + core

    ways = ((1, 0), (3, 1))
    rows_here = lbuf.at[:, aligned(core, 64), :]

    def start_one(i):
        m = far_m(own_parity, i)
        block = buf.at[m, part]
        there = prow.at[u, m]
        for k, n in ways + (((2, 2),) if i >= DIRECT else ()):
            pole, grid = at_x(k)
            remote(block, block, xg_send, xg_recv.at[n, i], pole, grid).start()
            remote(block, there, yg_send, yg_recv.at[n, i], at_y(k), g).start()
        remote(block, there, cg_send, cg_recv, partner, g).start()
        prow[u, m] = buf[m, part]

    def pass_one(i):
        m = far_m(own_parity, i)
        for k, n in ((3, 0), (1, 1)):
            ref = buf.at[far_m(x_own(k), i), x_part(k)]
            wait_in(ref, xg_recv.at[n, i])
            if i < DIRECT and i % 2 == n:
                pole, grid = at_x(4 - k)
                remote(ref, ref, xg_send, xg_recv.at[2, i], pole, grid).start()
        for k, n in ((3, 0), (1, 1)):
            ref = prow.at[y_part(k), m]
            wait_in(ref, yg_recv.at[n, i])
            if i < DIRECT and i % 2 == n:
                remote(ref, ref, yg_send, yg_recv.at[2, i], at_y(4 - k), g).start()

    def arrived(i):
        from_z(far_m(own_parity, i), buf.at[far_m(own_parity, i), part], pz_recv)

    for i in range(4):
        arrived(i)
        start_one(i)
    for n, rows in ((0, slice(0, 4)), (1, slice(4, 8))):
        wait_in(l_of(2, rows), ly_recv.at[2 + n])
    remote(rows_here, rows_here, lc_send, lc_recv, partner, g).start()
    for i in range(4, 8):
        pass_one(i - 4)
        arrived(i)
        start_one(i)
    for i in range(4, 8):
        pass_one(i)

    def send_cr(k):
        came = prow.at[y_part(k)]
        remote(came, came, cr_send, cr_recv, partner, g).start()

    send_cr(3)
    send_cr(1)
    for i in range(8):
        wait_in(buf.at[far_m(x_own(2), i), x_part(2)], xg_recv.at[2, i])
    for i in range(8):
        wait_in(prow.at[y_part(2), far_m(own_parity, i)], yg_recv.at[2, i])
    send_cr(2)
    small.wait()
    wait_in(rows_here, lc_recv)

    @pl.when(z != p)
    def _():
        wait_in(wtb, w_recv)

    wr = wtb[0:1, :]
    wi = wtb[1:2, :]
    off_place = off.at[0, :, :, aligned(u, 128)]

    def send_home(i):
        m = lax.rem(z + 16 - jnp.where(own_parity == 0, HOME[0][i], HOME[1][i]), 16) // 2
        remote(xb.at[m], off_place, r_send, o_recv, z, 2 * (2 * m + parity) + 1 - xl).start()

    for m in range(8):
        rows = []
        for k in range(8):
            j = ancb_s[m, 0, k]
            rows.append(jnp.concatenate([buf[j // 4, j % 4, 0], buf[j // 4, j % 4, 1]], axis=1))
        both = jnp.dot(lbuf[m], jnp.concatenate(rows, axis=0), preferred_element_type=F32)
        real = both[64:, 128:] - both[:64, :128]
        imag = -(both[:64, 128:] + both[64:, :128])
        xb[m, 0] = real.astype(BF16)
        xb[m, 1] = imag.astype(BF16)
        term = jnp.concatenate([wr * real - wi * imag, -wr * imag - wi * real], axis=0).T
        high = term.astype(BF16)
        yt[0:128, 128 * m : 128 * m + 128] = high
        yt[128:256, 128 * m : 128 * m + 128] = (term - high.astype(F32)).astype(BF16)

    for i in range(HELD):
        send_home(i)
    wait_in(prow.at[0], cg_recv)
    wait_in(prow.at[0:3], cr_recv)
    for n in range(4):
        columns = jnp.concatenate([prow[2 * n].reshape(1024, 128), prow[2 * n + 1].reshape(1024, 128)], axis=1)
        two = jnp.dot(yt[...], columns, preferred_element_type=F32)
        one = two[:128] + two[128:]
        d[4 * n : 4 * n + 2] = one[:, :128].T.reshape(2, 64, 128)
        d[4 * n + 2 : 4 * n + 4] = one[:, 128:].T.reshape(2, 64, 128)

    for h in range(2):
        for k in (2, 1, 3):
            pole, grid = at_x(k)
            there = pl.ds(pl.multiple_of(lax.rem(x + k, 4) * 16 + 8 * h, 8), 8)
            remote(d.at[:, there], rx.at[h, k - 1], xr_send, xr_recv.at[h], pole, grid).start()

    for h in range(2):
        wait_in(rx.at[h], xr_recv.at[h])
        here = pl.ds(pl.multiple_of(x * 16 + 8 * h, 8), 8)
        fb[h] = d[:, here] + rx[h, 0] + rx[h, 1] + rx[h, 2]

        def send_z(n):
            to = lax.rem(z + jnp.where(n % 2 == 0, 8 + n // 2, 7 - n // 2), 16)
            remote(fb.at[h, to], rz.at[h, z], z_send.at[h], z_recv.at[h], p, 2 * to + xl).start()

        each(15, send_z)
    for i in range(HELD, 8):
        send_home(i)

    @pl.when(xl == xh)
    def _():
        wait_in(dg.at[0:15], g_recv)
        wait_out(dg.at[0:15], g_send)

    @pl.when(xl != xh)
    def _():
        wait_in(dg, g_recv)
        wait_out(dg, g_send)

    wait_out(left, l_send)
    wait_out(panel, p_send)

    @pl.when(xh == 0)
    def _():
        for n in range(2):
            wait_out(ar, h_send.at[n])

    @pl.when(z == p)
    def _():
        def done_w(q):
            @pl.when(q != p)
            def _():
                wait_out(wt, w_send.at[q])

        each(16, done_w)

    def done_a(n):
        @pl.when(2 * n + pole_core != z)
        def _():
            wait_out(ar, a_send.at[n])

    each(8, done_a)

    wait_out(pr.at[0:2], pz_send.at[1])
    wait_out(pr.at[0:4], pz_send.at[2])
    wait_out(lbuf.at[:, 0:64, 0:256], ly_send.at[0])
    wait_out(lbuf.at[:, 0:64, 0:128], ly_send.at[1])
    wait_out(rows_here, lc_send)
    wait_out(prow.at[0:3], xg_send)
    wait_out(prow.at[0:3], yg_send)
    wait_out(prow.at[0], cg_send)
    wait_out(prow.at[0:3], cr_send)
    wait_out(rx, xr_send)

    total = dg[0]
    for n in range(1, 16):
        total = total + dg[n]
    for h in range(2):
        rz[h, z] = fb[h, z]
        wait_in(rz.at[h, 0:15], z_recv.at[h])
        minus = rz[h, 0]
        for n in range(1, 16):
            minus = minus + rz[h, n]
        res[8 * h : 8 * h + 8] = total[8 * h : 8 * h + 8] - minus

    place = dens.at[aligned(xl, 16), aligned(u, 128)]

    def send_n(k):
        n = lax.rem(p + k, 16)

        @pl.when(other(n, 2 * z + xh))
        def _():
            remote(res, place, n_send, n_recv, n, 2 * z + xh).start()

    each(16, send_n)

    @pl.when(xl == xh)
    def _():
        copy = pltpu.make_async_copy(res, place, one_sem.at[2])
        copy.start()
        copy.wait()

    wait_out(xb, r_send)
    for h in range(2):
        wait_out(fb.at[h, 0:15], z_send.at[h])

    @pl.when(xl == xh)
    def _():
        wait_out(dg.at[0:15], n_send)
        wait_in(dg.at[0:15], n_recv)

    @pl.when(xl != xh)
    def _():
        wait_out(dg, n_send)
        wait_in(dg, n_recv)

    wait_in(xb, o_recv)


def hand_over(off_h, dens_h, off, dens, off_v, dens_v, sem):
    ways = [(off_h, off_v, off), (dens_h, dens_v, dens)]
    first = [pltpu.make_async_copy(a, b, sem.at[0, n]) for n, (a, b, _) in enumerate(ways)]
    second = [pltpu.make_async_copy(b, c, sem.at[1, n]) for n, (_, b, c) in enumerate(ways)]
    for copy in first:
        copy.start()
    for a, b in zip(first, second):
        a.wait()
        b.start()
    for copy in second:
        copy.wait()


def shards(panel, inverse_blocks, diag_inverse, ancestors, pole_index, weight_table):
    vmem = pl.BlockSpec(memory_space=pltpu.VMEM)
    smem = pl.BlockSpec(memory_space=pltpu.SMEM)
    hbm = pl.BlockSpec(memory_space=pl.ANY)
    dma = pltpu.SemaphoreType.DMA
    scratch = [
        pltpu.VMEM((1, 2, 64, 1024), BF16),
        pltpu.VMEM((1, 1, 8, 2, 64, 64), BF16),
        pltpu.VMEM((1, 32, 2048), F32),
        pltpu.VMEM((128, 512), BF16),
        pltpu.VMEM((8, 128), F32),
        pltpu.VMEM((1, 8), jnp.int32),
        pltpu.VMEM((8, 2, 64, 128), BF16),
        pltpu.VMEM((8, 64, 128), BF16),
        pltpu.VMEM((8, 4, 2, 64, 128), BF16),
        pltpu.VMEM((8, 128, 512), BF16),
        pltpu.VMEM((8, 1, 8), jnp.int32),
        pltpu.SMEM((8, 1, 8), jnp.int32),
        pltpu.VMEM((8, 128), F32),
        pltpu.VMEM((8, 8, 2, 64, 128), BF16),
        pltpu.VMEM((8, 2, 64, 128), BF16),
        pltpu.VMEM((256, 1024), BF16),
        pltpu.VMEM((16, 64, 128), F32),
        pltpu.VMEM((2, 3, 16, 8, 128), F32),
        pltpu.VMEM((2, 16, 8, 128), F32),
        pltpu.VMEM((2, 16, 8, 128), F32),
        pltpu.VMEM((8, 32, 128), F32),
        pltpu.VMEM((16, 16, 128), F32),
        pltpu.VMEM((16, 128), F32),
        pltpu.SemaphoreType.REGULAR((3,)), dma((3,)), dma((3,)),
        dma, dma((8,)), dma, dma((8,)), dma((2,)), dma, dma((3,)), dma((8,)), dma, dma((8,)), dma((8,)), dma((8,)), dma((16,)), dma,
        dma, dma((3, 8)), dma, dma((3, 8)), dma, dma, dma, dma,
        dma((2,)), dma((4,)), dma, dma,
        dma, dma, dma, dma, dma, dma((2,)), dma((2,)), dma((2,)), dma, dma,
    ]
    results = pl.pallas_call(
        kernel,
        out_shape=(
            jax.ShapeDtypeStruct(panel.shape, BF16),
            jax.ShapeDtypeStruct((32, 1024), F32),
        ),
        in_specs=[vmem, smem, smem, hbm, hbm, hbm],
        out_specs=(hbm, hbm),
        scratch_shapes=scratch,
        compiler_params=pltpu.CompilerParams(
            collective_id=1, has_side_effects=True, vmem_limit_bytes=VMEM
        ),
    )(ancestors, pole_index, weight_table.T, panel, inverse_blocks, diag_inverse)
    return pl.pallas_call(
        hand_over,
        out_shape=(
            jax.ShapeDtypeStruct(panel.shape, BF16),
            jax.ShapeDtypeStruct((32, 1024), F32),
        ),
        in_specs=[hbm, hbm],
        out_specs=(hbm, hbm),
        scratch_shapes=[pltpu.VMEM(panel.shape, BF16), pltpu.VMEM((32, 1024), F32), dma((2, 2))],
        compiler_params=pltpu.CompilerParams(vmem_limit_bytes=VMEM),
    )(*results)


def solution(mesh):
    placed = (
        P("pole", None, "grid", None),
        P("pole", "grid", None, None, None, None),
        P("pole", "grid", None),
        P("grid", None),
        P("pole"),
        P(),
    )
    return jax.shard_map(
        shards,
        mesh=mesh,
        in_specs=placed,
        out_specs=(P("pole", None, "grid", None), P("grid", None)),
        check_vma=False,
    )
```
